128 devices in a mesh: slab: 32 (over x, z, core), pencil: 4 (over y).
Axes of the slice: x: 4, y: 4, z: 4, core: 2. Of those that a mesh axis runs over, the one named last changes fastest.
Arguments:
- basis: bfloat16 [88, 256, 128, 128], P(None, 'slab', 'pencil'), may hold values from -6 to 6
- image: bfloat16 [88, 256, 128, 128], P(None, 'slab', 'pencil'), may hold values from -6.3 to 6.3
- material: int32 [256, 128, 128], P('slab', 'pencil'), may hold values from 0 to 3
- picked: int32 [32], replicated, may hold values from 0 to 87, as said below
Outputs:
- recycle_out: float32 [32, 256, 128, 128], P(None, 'slab', 'pencil')
- images_out: float32 [32, 256, 128, 128], P(None, 'slab', 'pencil')
The draws below stay inside these ranges and needn't reach their ends.
Inputs may be any that keep to these rules, and one draw needn't show every extreme that they name: `picked`: 32 distinct column numbers.
All inputs are finite; a program needn't handle non-finite values.
Results may differ from the reference program's by a relative error of at most 0.0061.
Values may be sent and summed in bfloat16 or wider, within the bound.
No kernel may reach another device: no remote copies, remote signals or barrier semaphores. Data moves between devices by JAX's collectives and lax.ppermute only.
A program may use at most 128 MiB of HBM per device.

```python
import jax
import jax.numpy as jnp
from jax import lax

RECYCLE = 32
COLS = 88
GX = 128
NY = 128
NZ = 256


def draw_image(key, part):
    key = jax.random.fold_in(key, 11)
    noise_key = jax.random.fold_in(key, 0)
    values = jax.random.truncated_normal(noise_key, -3.9, 3.9, (COLS + 1, NZ, NY, GX), jnp.float32)
    return (values[1:] + 0.6 * values[:-1]).astype(jnp.bfloat16)


def draw_picked(key, part):
    key = jax.random.fold_in(key, 23)
    return jax.random.permutation(key, COLS)[:RECYCLE].astype(jnp.int32)


def box_field(key, column):
    column_key = jax.random.fold_in(key, column)
    raw_values = jax.random.randint(column_key, (NZ + 8, NY + 8, GX + 8), -8, 9).astype(jnp.float32)
    along_z = raw_values[0:NZ]
    for offset in range(1, 9):
        along_z = along_z + raw_values[offset:offset + NZ]
    along_y = along_z[:, 0:NY]
    for offset in range(1, 9):
        along_y = along_y + along_z[:, offset:offset + NY]
    along_x = along_y[:, :, 0:GX]
    for offset in range(1, 9):
        along_x = along_x + along_y[:, :, offset:offset + GX]
    return along_x


def draw_basis(key, part):
    key = jax.random.fold_in(key, 31)
    field_key = jax.random.fold_in(key, 0)
    unit_scale = 0.0012966
    factors = jnp.full((COLS,), unit_scale, jnp.float32)
    first = box_field(field_key, 0)

    def advance(previous, inputs):
        column, factor = inputs
        current = box_field(field_key, column)
        mixed = (current * 5.0 + previous * 3.0) * factor
        return (current, jnp.clip(mixed, -6.0, 6.0).astype(jnp.bfloat16))
    columns_index = jnp.arange(1, COLS + 1).astype(jnp.int32)
    _, result = lax.scan(advance, first, (columns_index, factors))
    return result


def draw_material(key, part):
    key = jax.random.fold_in(key, 41)
    which_key, kind_key = jax.random.split(key)
    which = jax.random.randint(which_key, (NZ, NY, GX), 0, 10)
    other = jax.random.randint(kind_key, (NZ, NY, GX), 1, 4)
    return jnp.where(which == 0, other, 0).astype(jnp.int32)


def setup_inputs(seed: int = 0) -> dict:
    key_list = jax.random.split(jax.random.key(seed), 5)
    basis = draw_basis(jax.random.fold_in(key_list[4], 71), 0)
    image = draw_image(jax.random.fold_in(key_list[4], 71), 0)
    material = draw_material(jax.random.fold_in(key_list[4], 71), 0)
    picked = draw_picked(jax.random.fold_in(key_list[4], 71), 0)
    return {"basis": basis, "image": image, "material": material, "picked": picked}


def squared_wave(material):
    return jnp.where(material == 0, 0.3, jnp.where(material == 1, 0.9, jnp.where(material == 2, 1.6, 2.5))).astype(jnp.float32)

def stencil(padded, material):
    padded = jnp.pad(padded, ((0, 0), (0, 0), (0, 0), (1, 1)))
    center = padded[:, 1:-1, 1:-1, 1:-1]
    beside = padded[:, 2:, 1:-1, 1:-1] + padded[:, :-2, 1:-1, 1:-1]
    beside = beside + padded[:, 1:-1, 2:, 1:-1] + padded[:, 1:-1, :-2, 1:-1]
    beside = beside + padded[:, 1:-1, 1:-1, 2:] + padded[:, 1:-1, 1:-1, :-2]
    return (6.0 - squared_wave(material)) * center - beside

def harmonic_columns(gram_matrix, cross_matrix, picked):
    lower_factor = jnp.linalg.cholesky(gram_matrix)
    halfway = lax.linalg.triangular_solve(lower_factor, cross_matrix, left_side=True, lower=True)
    coefficients = lax.linalg.triangular_solve(lower_factor, halfway, left_side=True, lower=True, transpose_a=True)
    return jnp.take(coefficients, picked, axis=1).astype(jnp.bfloat16)

def inverse_factor(normal_matrix):
    lower_factor = jnp.linalg.cholesky(normal_matrix)
    identity = jnp.eye(normal_matrix.shape[0], dtype=normal_matrix.dtype)
    return lax.linalg.triangular_solve(lower_factor, identity, left_side=True, lower=True)

def reference(basis, image, material, picked):
    flat_basis = basis.reshape(COLS, -1)
    flat_image = image.reshape(COLS, -1)
    gram_matrix = jnp.dot(flat_image.astype(jnp.float32), flat_image.T.astype(jnp.float32), preferred_element_type=jnp.float32)
    cross_matrix = jnp.dot(flat_image.astype(jnp.float32), flat_basis.T.astype(jnp.float32), preferred_element_type=jnp.float32)
    chosen = harmonic_columns(gram_matrix, cross_matrix, picked)
    recycle = jnp.dot(chosen.T.astype(jnp.float32), flat_basis.astype(jnp.float32), preferred_element_type=jnp.float32).reshape(RECYCLE, NZ, NY, GX)
    padded = jnp.pad(recycle, ((0, 0), (1, 1), (1, 1), (0, 0)))
    applied = stencil(padded, material)
    flat_applied = applied.reshape(RECYCLE, -1)
    flat_recycle = recycle.reshape(RECYCLE, -1)
    normal_matrix = jnp.dot(flat_applied.astype(jnp.float32), flat_applied.T.astype(jnp.float32), precision=lax.Precision.HIGHEST, preferred_element_type=jnp.float32) / (NZ * NY * GX)
    inverse = inverse_factor(normal_matrix)
    recycle_out = jnp.dot(inverse.astype(jnp.float32), flat_recycle.astype(jnp.float32), precision=lax.Precision.HIGHEST, preferred_element_type=jnp.float32)
    images_out = jnp.dot(inverse.astype(jnp.float32), flat_applied.astype(jnp.float32), precision=lax.Precision.HIGHEST, preferred_element_type=jnp.float32)
    return (recycle_out.reshape(RECYCLE, NZ, NY, GX), images_out.reshape(RECYCLE, NZ, NY, GX))
```

```python
import jax
import jax.numpy as jnp
from jax import lax
from jax.experimental import pallas as pl
from jax.experimental.pallas import tpu as pltpu
from jax.sharding import PartitionSpec as P

F32 = jnp.float32
BF16 = jnp.bfloat16
CELLS = 4194304.0
PITCH = 44
NT = (((1,), (1,)), ((), ()))
TN = (((0,), (0,)), ((), ()))
MIB = 2**20


def gram_kernel(picked, image, basis, sums, turned, image_slab, basis_slab, rows, sems):
    columns, depth, height, width = image.shape
    count = picked.shape[0]
    total = columns + count
    slots = image_slab.shape[0]

    def copies(z, slot):
        return (
            pltpu.make_async_copy(image.at[:, z], image_slab.at[slot], sems.at[slot, 0]),
            pltpu.make_async_copy(basis.at[:, z], basis_slab.at[slot], sems.at[slot, 1]),
        )

    for z in range(slots - 1):
        for copy in copies(z, z):
            copy.start()
    sums[...] = jnp.zeros_like(sums)

    def step(z, _):
        slot = lax.rem(z, slots)

        @pl.when(z + slots - 1 < depth)
        def _():
            for copy in copies(z + slots - 1, lax.rem(z + slots - 1, slots)):
                copy.start()

        for copy in copies(z, slot):
            copy.wait()
        for c in range(columns):
            rows[c * PITCH : c * PITCH + height] = image_slab[slot, c].astype(F32)
        for c in range(count):
            at = (columns + c) * PITCH
            rows[at : at + height] = basis_slab[slot, picked[c]].astype(F32)
        for y in range(0, height, 16):
            turned[z, y : y + 16] = jnp.swapaxes(basis_slab[slot, :, y : y + 16, :], 0, 1)
        both = jnp.concatenate(
            [rows[pl.ds(y, total, stride=PITCH), :].astype(BF16) for y in range(height)], 1
        )
        part = lax.dot_general(both, both[:columns], NT, preferred_element_type=F32)
        sums[:, :columns] += part
        return 0

    lax.fori_loop(0, depth, step, 0)


def coefficient(material):
    squared = jnp.where(
        material == 0, 0.3, jnp.where(material == 1, 0.9, jnp.where(material == 2, 1.6, 2.5))
    ).astype(F32)
    return 6.0 - squared


def beside_in_row(row, first, last):
    width = row.shape[1]
    up = jnp.where(first, 0.0, pltpu.roll(row, 1, 1))
    down = jnp.where(last, 0.0, pltpu.roll(row, width - 1, 1))
    return up + down


def normal_kernel(
    sums, turned, material, z_low, z_high, y_low, y_high, packed, field, gram, sems
):
    depth, height, columns, width = turned.shape
    count = sums.shape[0] - columns
    copies = [
        pltpu.make_async_copy(turned.at[z], field.at[z + 1, 1 : height + 1], sems.at[z])
        for z in range(depth)
    ]
    for copy in copies:
        copy.start()
    for y in range(0, height, 16):
        field[0, y + 1 : y + 17] = jnp.swapaxes(z_low[:, y : y + 16, :], 0, 1)
        field[depth + 1, y + 1 : y + 17] = jnp.swapaxes(z_high[:, y : y + 16, :], 0, 1)
    low = jnp.swapaxes(y_low[...], 0, 1)
    high = jnp.swapaxes(y_high[...], 0, 1)
    for z in range(depth):
        field[z + 1, 0] = low[z]
        field[z + 1, height + 1] = high[z]
    gram[...] = jnp.zeros_like(gram)
    for copy in copies:
        copy.wait()
    lane = lax.broadcasted_iota(jnp.int32, (columns, width), 1)
    first, last = lane == 0, lane == width - 1

    def step(z, _):
        scale = coefficient(material[z])
        highs, lows = [], []
        for y in range(height):
            row = field[z + 1, y + 1].astype(F32)
            beside = field[z, y + 1].astype(F32) + field[z + 2, y + 1].astype(F32)
            beside = beside + (field[z + 1, y].astype(F32) + field[z + 1, y + 2].astype(F32))
            beside = beside + beside_in_row(row, first, last)
            image = scale[y : y + 1, :] * row - beside
            rounded = image.astype(BF16)
            highs.append(rounded)
            lows.append((image - rounded.astype(F32)).astype(BF16))
        rounded = jnp.concatenate(highs, 1)
        both = jnp.concatenate([rounded, jnp.concatenate(lows, 1)], 0)
        gram[...] += lax.dot_general(both, rounded, NT, preferred_element_type=F32)
        return 0

    lax.fori_loop(0, depth, step, 0)
    side = jnp.zeros((columns, 128 - columns), F32)
    foot = jnp.zeros((128 - columns, 128), F32)
    cross = jnp.concatenate([gram[columns:], side], 1)
    cross_t = jnp.concatenate([cross, foot], 0).T[:columns]
    normal = jnp.concatenate([gram[:columns], side], 1) + cross + cross_t
    col = lax.broadcasted_iota(jnp.int32, (columns, 128), 1)
    line = lax.broadcasted_iota(jnp.int32, (columns, 128), 0)
    diagonal = jnp.sum(jnp.where(line == col, normal, 0.0), axis=1, keepdims=True)
    grams = sums[:columns]
    picked_t = jnp.concatenate(
        [jnp.concatenate([sums[columns:], jnp.zeros((count, 128 - columns), F32)], 1),
         jnp.zeros((128 - count, 128), F32)], 0
    ).T[:columns]
    placed = pltpu.roll(picked_t, columns, 1)
    grams = jnp.concatenate([grams, side], 1)
    out = jnp.where(line >= col, grams, normal)
    out = jnp.where(col >= columns, placed, out)
    packed[...] = jnp.where(col == columns + count, diagonal, out)


def spread(row, lane):
    return jnp.broadcast_to(row[:, lane : lane + 1], row.shape)


def eliminate(blocks, panel, followers):
    base = 8 * panel
    wide = blocks[panel].shape
    rows = [jnp.broadcast_to(blocks[panel][i : i + 1, :], wide) for i in range(8)]
    heads = [[spread(rows[i], base + j) for j in range(8)] for i in range(8)]
    forward, pivots = [], []
    for k in range(8):
        forward.append(rows[k])
        pivots.append(heads[k][k])
        inverse = 1.0 / heads[k][k]
        rows[k] = rows[k] * inverse
        for j in range(k + 1, 8):
            heads[k][j] = heads[k][j] * inverse
        for i in range(8):
            if i == k:
                continue
            factor = heads[i][k]
            rows[i] = rows[i] - factor * rows[k]
            for j in range(k + 1, 8):
                heads[i][j] = heads[i][j] - factor * heads[k][j]
    for i in followers:
        block = blocks[i]
        for j in range(8):
            block = block - spread(blocks[i], base + j) * rows[j]
        blocks[i] = block
    return rows, forward, pivots


def stacked(rows):
    line = lax.broadcasted_iota(jnp.int32, rows[0].shape, 0)
    out = rows[0]
    for i in range(1, 8):
        out = jnp.where(line == i, rows[i], out)
    return out


def combination(packed, columns, count):
    exact = lax.Precision.HIGHEST
    shape = (128, 128)
    col = lax.broadcasted_iota(jnp.int32, shape, 1)
    line = lax.broadcasted_iota(jnp.int32, shape, 0)
    full = jnp.concatenate([packed, jnp.zeros((128 - columns, 128), F32)], 0)
    flipped = full.T
    grams = jnp.where(line >= col, full, flipped)
    grams = jnp.where(col >= columns, full, grams)
    diagonal = jnp.broadcast_to(full[:, columns + count : columns + count + 1], shape)
    normal = jnp.where(line < col, full, flipped)
    normal = jnp.where(line == col, diagonal, normal)
    normal = jnp.where((col < columns) & (line < columns), normal, 0.0)
    blocks = [grams[8 * i : 8 * i + 8] for i in range(columns // 8)]
    for panel in range(len(blocks)):
        rest = [i for i in range(len(blocks)) if i != panel]
        rows, _, _ = eliminate(blocks, panel, rest)
        blocks[panel] = stacked(rows)
    solved = jnp.concatenate(blocks + [jnp.zeros((128 - columns, 128), F32)], 0)
    solved = pltpu.roll(solved, 128 - columns, 1)
    chosen = jnp.where(col < count, solved, 0.0).astype(BF16).astype(F32)
    chosen_t = chosen.T
    product = jnp.dot(normal, chosen, precision=exact, preferred_element_type=F32)
    normal = jnp.dot(chosen_t, product, precision=exact, preferred_element_type=F32)
    normal = normal[:count] * (1.0 / CELLS)
    joined = jnp.where(col[:count] < count, normal, pltpu.roll(chosen_t[:count], count, 1))
    blocks = [joined[8 * i : 8 * i + 8] for i in range(count // 8)]
    for panel in range(len(blocks)):
        rest = range(panel + 1, len(blocks))
        _, forward, pivots = eliminate(blocks, panel, rest)
        blocks[panel] = stacked([r * lax.rsqrt(d) for r, d in zip(forward, pivots)])
    return pltpu.roll(jnp.concatenate(blocks, 0), 128 - count, 1)[:, :columns]


def update_kernel(
    packed, turned, material, z_low, z_high, y_low, y_high, recycle, images,
    field, planes, first_out, second_out, load_sems, store_sems,
):
    depth, height, columns, width = turned.shape
    count = recycle.shape[0]
    loads = [
        pltpu.make_async_copy(turned.at[z], field.at[z + 1], load_sems.at[z])
        for z in range(depth)
    ]
    for copy in loads:
        copy.start()
    for y in range(0, height, 16):
        field[0, y : y + 16] = jnp.swapaxes(z_low[:, y : y + 16, :], 0, 1)
        field[depth + 1, y : y + 16] = jnp.swapaxes(z_high[:, y : y + 16, :], 0, 1)
    weights = combination(packed[...], columns, count)
    rounded = weights.astype(BF16)
    both = jnp.concatenate([rounded, (weights - rounded.astype(F32)).astype(BF16)], 0)

    def combine(row):
        part = jnp.dot(both, row, preferred_element_type=F32)
        return part[:count] + part[count:]

    low = jnp.swapaxes(y_low[...], 0, 1)
    high = jnp.swapaxes(y_high[...], 0, 1)
    low = combine(jnp.concatenate([low[z] for z in range(depth)], 1))
    high = combine(jnp.concatenate([high[z] for z in range(depth)], 1))
    for z in range(depth):
        planes[z + 1, 0] = low[:, z * width : (z + 1) * width]
        planes[z + 1, height + 1] = high[:, z * width : (z + 1) * width]
    for copy in loads:
        copy.wait()

    def fill(z):
        plane = combine(jnp.concatenate([field[z, y] for y in range(height)], 1))
        for y in range(height):
            planes[z, y + 1] = plane[:, y * width : (y + 1) * width]

    def stores(z, slot):
        return (
            pltpu.make_async_copy(first_out.at[slot], recycle.at[:, z], store_sems.at[slot, 0]),
            pltpu.make_async_copy(second_out.at[slot], images.at[:, z], store_sems.at[slot, 1]),
        )

    fill(0)
    fill(1)
    lane = lax.broadcasted_iota(jnp.int32, (count, width), 1)
    first, last = lane == 0, lane == width - 1

    def step(z, _):
        slot = lax.rem(z, 2)
        fill(z + 2)

        @pl.when(z >= 2)
        def _():
            for copy in stores(z - 2, slot):
                copy.wait()

        scale = coefficient(material[z])
        one = first_out.at[slot].reshape(count * height, width)
        two = second_out.at[slot].reshape(count * height, width)
        for y in range(height):
            row = planes[z + 1, y + 1]
            beside = planes[z, y + 1] + planes[z + 2, y + 1]
            beside = beside + (planes[z + 1, y] + planes[z + 1, y + 2])
            beside = beside + beside_in_row(row, first, last)
            one[pl.ds(y, count, stride=height), :] = row
            two[pl.ds(y, count, stride=height), :] = scale[y : y + 1, :] * row - beside
        for copy in stores(z, slot):
            copy.start()
        return 0

    lax.fori_loop(0, depth, step, 0)
    for z in (depth - 2, depth - 1):
        for copy in stores(z, z % 2):
            copy.wait()


def device_sum(value):
    def shifted(axis, perm):
        return lax.ppermute(value, axis, perm)

    slabs = range(32)
    value = value + shifted("slab", [(i, i ^ 1) for i in slabs])
    for stride in (8, 2, 0):
        if stride:
            def move(i, d):
                place = (i // stride) % 4
                return i + ((place + d) % 4 - place) * stride
            axis, perms = "slab", [[(i, move(i, d)) for i in slabs] for d in (1, 2, 3)]
        else:
            axis = "pencil"
            perms = [[(i, (i + d) % 4) for i in range(4)] for d in (1, 2, 3)]
        left, opposite, right = [shifted(axis, perm) for perm in perms]
        value = (value + opposite) + (left + right)
    return value


def whole(memory=pltpu.VMEM):
    return pl.BlockSpec(memory_space=memory)


def local(basis, image, material, picked):
    columns, depth, height, width = basis.shape
    count = picked.shape[0]
    slabs, pencils = lax.axis_size("slab"), lax.axis_size("pencil")

    def neighbours(low_face, high_face, axis, size):
        up = [(i, i + 1) for i in range(size - 1)]
        down = [(j, i) for i, j in up]
        return lax.ppermute(high_face, axis, up), lax.ppermute(low_face, axis, down)

    z_low, z_high = neighbours(basis[:, 0], basis[:, depth - 1], "slab", slabs)
    y_low, y_high = neighbours(basis[:, :, 0], basis[:, :, height - 1], "pencil", pencils)

    sums, turned = pl.pallas_call(
        gram_kernel,
        in_specs=[whole(pltpu.SMEM), whole(pl.ANY), whole(pl.ANY)],
        out_specs=[whole(), whole()],
        out_shape=[
            jax.ShapeDtypeStruct((columns + count, columns), F32),
            jax.ShapeDtypeStruct((depth, height, columns, width), BF16),
        ],
        scratch_shapes=[
            pltpu.VMEM((3, columns, height, width), BF16),
            pltpu.VMEM((3, columns, height, width), BF16),
            pltpu.VMEM(((columns + count) * PITCH, width), F32),
            pltpu.SemaphoreType.DMA((3, 2)),
        ],
        compiler_params=pltpu.CompilerParams(vmem_limit_bytes=24 * MIB),
        cost_estimate=pl.CostEstimate(flops=2 * 10**9, bytes_accessed=17 * 10**6, transcendentals=0),
        name="gram",
    )(picked, image, basis)
    faces = (z_low, z_high, y_low, y_high)
    packed = pl.pallas_call(
        normal_kernel,
        in_specs=[whole(), whole(pl.ANY), whole(), whole(), whole(), whole(), whole()],
        out_specs=whole(),
        out_shape=jax.ShapeDtypeStruct((columns, 128), F32),
        scratch_shapes=[
            pltpu.VMEM((depth + 2, height + 2, columns, width), BF16),
            pltpu.VMEM((2 * columns, columns), F32),
            pltpu.SemaphoreType.DMA((depth,)),
        ],
        compiler_params=pltpu.CompilerParams(vmem_limit_bytes=24 * MIB),
        name="normal",
    )(sums, turned, material, *faces)
    packed = device_sum(packed)
    grid_shape = (count, depth, height, width)
    return pl.pallas_call(
        update_kernel,
        in_specs=[whole(), whole(pl.ANY), whole(), whole(), whole(), whole(), whole()],
        out_specs=[whole(pl.ANY), whole(pl.ANY)],
        out_shape=[jax.ShapeDtypeStruct(grid_shape, F32)] * 2,
        scratch_shapes=[
            pltpu.VMEM((depth + 2, height, columns, width), BF16),
            pltpu.VMEM((depth + 2, height + 2, count, width), F32),
            pltpu.VMEM((2, count, height, width), F32),
            pltpu.VMEM((2, count, height, width), F32),
            pltpu.SemaphoreType.DMA((depth,)),
            pltpu.SemaphoreType.DMA((2, 2)),
        ],
        compiler_params=pltpu.CompilerParams(vmem_limit_bytes=32 * MIB),
        name="update",
    )(packed, turned, material, *faces)


def solution(mesh):
    field = P(None, "slab", "pencil", None)
    return jax.shard_map(
        local,
        mesh=mesh,
        in_specs=(field, field, P("slab", "pencil", None), P()),
        out_specs=(field, field),
        check_vma=False,
    )
```

```python
import jax
import jax.numpy as jnp
from jax import lax
from jax.experimental import pallas as pl
from jax.experimental.pallas import tpu as pltpu
from jax.sharding import PartitionSpec as P

F32 = jnp.float32
BF16 = jnp.bfloat16
CELLS = 4194304.0
PITCH = 44
STEP = 40
NT = (((1,), (1,)), ((), ()))
TN = (((0,), (0,)), ((), ()))
MIB = 2**20


def turn_kernel(basis, turned, z_first, z_last, y_first, y_last, slab, sems):
    columns, depth, height, width = basis.shape
    slots = slab.shape[0]

    def load(z, slot):
        return pltpu.make_async_copy(basis.at[:, z], slab.at[slot], sems.at[slot])

    for z in range(slots - 1):
        load(z, z).start()

    def step(z, _):
        slot = lax.rem(z, slots)

        @pl.when(z + slots - 1 < depth)
        def _():
            load(z + slots - 1, lax.rem(z + slots - 1, slots)).start()

        load(z, slot).wait()
        for y in range(0, height, 16):
            part = jnp.swapaxes(slab[slot, :, y : y + 16, :], 0, 1)
            turned[z, y : y + 16] = part
            if y == 0:
                y_first[z] = part[0]
            if y + 16 == height:
                y_last[z] = part[15]
        return 0

    lax.fori_loop(0, depth, step, 0)
    z_first[...] = turned[0]
    z_last[...] = turned[depth - 1]


def gram_kernel(picked, image, basis, sums, image_slab, picked_slab, rows, sems, picked_sems):
    columns, depth, height, width = image.shape
    count = picked.shape[0]
    total = columns + count
    slots = image_slab.shape[0]

    def load(z, slot):
        return pltpu.make_async_copy(image.at[:, z], image_slab.at[slot], sems.at[slot])

    def load_picked(c):
        return pltpu.make_async_copy(basis.at[picked[c]], picked_slab.at[c], picked_sems.at[c])

    load(0, 0).start()
    for c in range(count):
        load_picked(c).start()
    for z in range(1, slots - 1):
        load(z, z).start()
    sums[...] = jnp.zeros_like(sums)
    for c in range(count):
        load_picked(c).wait()

    def step(z, _):
        slot = lax.rem(z, slots)

        @pl.when(z + slots - 1 < depth)
        def _():
            load(z + slots - 1, lax.rem(z + slots - 1, slots)).start()

        for c in range(count):
            at = (columns + c) * PITCH
            rows[at : at + height] = picked_slab[c, z].astype(F32)
        load(z, slot).wait()
        for c in range(columns):
            rows[c * PITCH : c * PITCH + height] = image_slab[slot, c].astype(F32)
        both = jnp.concatenate(
            [rows[pl.ds(y, total, stride=PITCH), :].astype(BF16) for y in range(height)], 1
        )
        sums[...] += lax.dot_general(both, both[:columns], NT, preferred_element_type=F32)
        return 0

    lax.fori_loop(0, depth, step, 0)


def coefficient(material):
    squared = jnp.where(
        material == 0, 0.3, jnp.where(material == 1, 0.9, jnp.where(material == 2, 1.6, 2.5))
    ).astype(F32)
    return 6.0 - squared


def beside_in_row(row, first, last):
    width = row.shape[1]
    up = jnp.where(first, 0.0, pltpu.roll(row, 1, 1))
    down = jnp.where(last, 0.0, pltpu.roll(row, width - 1, 1))
    return up + down


def normal_kernel(
    sums, turned, material, z_low, z_high, y_low, y_high, packed, field, kinds, gram, sems, kind_sem
):
    depth, height, columns, width = turned.shape
    count = sums.shape[0] - columns
    kind_load = pltpu.make_async_copy(material, kinds, kind_sem)
    loads = [pltpu.make_async_copy(z_low, field.at[0], sems.at[0])]
    for z in range(depth):
        loads.append(pltpu.make_async_copy(turned.at[z], field.at[z + 1], sems.at[z + 1]))
    loads.append(pltpu.make_async_copy(z_high, field.at[depth + 1], sems.at[depth + 1]))
    for copy in [kind_load] + loads:
        copy.start()
    gram[...] = jnp.zeros_like(gram)
    lane = lax.broadcasted_iota(jnp.int32, (columns, width), 1)
    first, last = lane == 0, lane == width - 1
    kind_load.wait()
    loads[0].wait()
    loads[1].wait()

    def step(z, _):
        @pl.when(z < depth - 1)
        def _():
            pltpu.make_async_copy(turned.at[z + 1], field.at[z + 2], sems.at[z + 2]).wait()

        @pl.when(z == depth - 1)
        def _():
            loads[depth + 1].wait()

        scale = coefficient(kinds[z])
        middle = [y_low[z].astype(F32), field[z + 1, 0].astype(F32)]
        highs, lows = [], []
        for y in range(height):
            after = y_high[z] if y == height - 1 else field[z + 1, y + 1]
            middle.append(after.astype(F32))
            row = middle[y + 1]
            beside = field[z, y].astype(F32) + field[z + 2, y].astype(F32)
            beside = beside + (middle[y] + middle[y + 2])
            beside = beside + beside_in_row(row, first, last)
            image = scale[y : y + 1, :] * row - beside
            rounded = image.astype(BF16)
            highs.append(rounded)
            lows.append((image - rounded.astype(F32)).astype(BF16))
        rounded = jnp.concatenate(highs, 1)
        both = jnp.concatenate([rounded, jnp.concatenate(lows, 1)], 0)
        gram[...] += lax.dot_general(both, rounded, NT, preferred_element_type=F32)
        return 0

    lax.fori_loop(0, depth, step, 0)
    side = jnp.zeros((columns, 128 - columns), F32)
    foot = jnp.zeros((128 - columns, 128), F32)
    cross = jnp.concatenate([gram[columns:], side], 1)
    cross_t = jnp.concatenate([cross, foot], 0).T[:columns]
    normal = jnp.concatenate([gram[:columns], side], 1) + cross + cross_t
    col = lax.broadcasted_iota(jnp.int32, (columns, 128), 1)
    line = lax.broadcasted_iota(jnp.int32, (columns, 128), 0)
    diagonal = jnp.sum(jnp.where(line == col, normal, 0.0), axis=1, keepdims=True)
    grams = sums[:columns]
    picked_t = jnp.concatenate(
        [jnp.concatenate([sums[columns:], jnp.zeros((count, 128 - columns), F32)], 1),
         jnp.zeros((128 - count, 128), F32)], 0
    ).T[:columns]
    placed = pltpu.roll(picked_t, columns, 1)
    grams = jnp.concatenate([grams, side], 1)
    out = jnp.where(line >= col, grams, normal)
    out = jnp.where(col >= columns, placed, out)
    packed[...] = jnp.where(col == columns + count, diagonal, out)


def spread(row, lane):
    return jnp.broadcast_to(row[:, lane : lane + 1], row.shape)


def eliminate(blocks, panel, followers):
    base = 8 * panel
    wide = blocks[panel].shape
    rows = [jnp.broadcast_to(blocks[panel][i : i + 1, :], wide) for i in range(8)]
    heads = [[spread(rows[i], base + j) for j in range(8)] for i in range(8)]
    forward, pivots = [], []
    for k in range(8):
        forward.append(rows[k])
        pivots.append(heads[k][k])
        inverse = 1.0 / heads[k][k]
        rows[k] = rows[k] * inverse
        for j in range(k + 1, 8):
            heads[k][j] = heads[k][j] * inverse
        for i in range(8):
            if i == k:
                continue
            factor = heads[i][k]
            rows[i] = rows[i] - factor * rows[k]
            for j in range(k + 1, 8):
                heads[i][j] = heads[i][j] - factor * heads[k][j]
    for i in followers:
        block = blocks[i]
        for j in range(8):
            block = block - spread(blocks[i], base + j) * rows[j]
        blocks[i] = block
    return rows, forward, pivots


def stacked(rows):
    line = lax.broadcasted_iota(jnp.int32, rows[0].shape, 0)
    out = rows[0]
    for i in range(1, 8):
        out = jnp.where(line == i, rows[i], out)
    return out


def combination(packed, columns, count):
    exact = lax.Precision.HIGHEST
    shape = (128, 128)
    col = lax.broadcasted_iota(jnp.int32, shape, 1)
    line = lax.broadcasted_iota(jnp.int32, shape, 0)
    full = jnp.concatenate([packed, jnp.zeros((128 - columns, 128), F32)], 0)
    flipped = full.T
    grams = jnp.where(line >= col, full, flipped)
    grams = jnp.where(col >= columns, full, grams)
    diagonal = jnp.broadcast_to(full[:, columns + count : columns + count + 1], shape)
    normal = jnp.where(line < col, full, flipped)
    normal = jnp.where(line == col, diagonal, normal)
    normal = jnp.where((col < columns) & (line < columns), normal, 0.0)
    blocks = [grams[8 * i : 8 * i + 8] for i in range(columns // 8)]
    for panel in range(len(blocks)):
        rest = [i for i in range(len(blocks)) if i != panel]
        rows, _, _ = eliminate(blocks, panel, rest)
        blocks[panel] = stacked(rows)
    solved = jnp.concatenate(blocks + [jnp.zeros((128 - columns, 128), F32)], 0)
    solved = pltpu.roll(solved, 128 - columns, 1)
    chosen = jnp.where(col < count, solved, 0.0).astype(BF16).astype(F32)
    chosen_t = chosen.T
    product = jnp.dot(normal, chosen, precision=exact, preferred_element_type=F32)
    normal = jnp.dot(chosen_t, product, precision=exact, preferred_element_type=F32)
    normal = normal[:count] * (1.0 / CELLS)
    joined = jnp.where(col[:count] < count, normal, pltpu.roll(chosen_t[:count], count, 1))
    blocks = [joined[8 * i : 8 * i + 8] for i in range(count // 8)]
    for panel in range(len(blocks)):
        rest = range(panel + 1, len(blocks))
        _, forward, pivots = eliminate(blocks, panel, rest)
        blocks[panel] = stacked([r * lax.rsqrt(d) for r, d in zip(forward, pivots)])
    return pltpu.roll(jnp.concatenate(blocks, 0), 128 - count, 1)[:, :columns]


def update_kernel(
    packed, turned, material, z_low, z_high, y_low, y_high, recycle, images,
    field, kinds, planes, first_out, second_out, load_sems, kind_sem, store_sems,
):
    depth, height, columns, width = turned.shape
    count = recycle.shape[0]
    loads = [pltpu.make_async_copy(z_low, field.at[0], load_sems.at[0])]
    for z in range(depth):
        loads.append(pltpu.make_async_copy(turned.at[z], field.at[z + 1], load_sems.at[z + 1]))
    loads.append(pltpu.make_async_copy(z_high, field.at[depth + 1], load_sems.at[depth + 1]))
    loads.append(pltpu.make_async_copy(material, kinds, kind_sem))
    for copy in loads:
        copy.start()
    weights = combination(packed[...], columns, count)
    rounded = weights.astype(BF16)
    both = jnp.concatenate([rounded, (weights - rounded.astype(F32)).astype(BF16)], 0)

    def combine(row):
        part = jnp.dot(both, row, preferred_element_type=F32)
        return part[:count] + part[count:]

    low = combine(jnp.concatenate([y_low[z] for z in range(depth)], 1))
    high = combine(jnp.concatenate([y_high[z] for z in range(depth)], 1))
    for z in range(depth):
        planes[z + 1, 0] = low[:, z * width : (z + 1) * width]
        planes[z + 1, height + 1] = high[:, z * width : (z + 1) * width]
    for copy in loads:
        copy.wait()

    def fill(z):
        plane = combine(jnp.concatenate([field[z, y] for y in range(height)], 1))
        for y in range(height):
            planes[z, y + 1] = plane[:, y * width : (y + 1) * width]

    def stores(z, slot):
        return (
            pltpu.make_async_copy(first_out.at[slot, :, :height], recycle.at[:, z], store_sems.at[slot, 0]),
            pltpu.make_async_copy(second_out.at[slot, :, :height], images.at[:, z], store_sems.at[slot, 1]),
        )

    fill(0)
    fill(1)
    lane = lax.broadcasted_iota(jnp.int32, (count, width), 1)
    first, last = lane == 0, lane == width - 1

    def step(z, _):
        slot = lax.rem(z, 2)
        fill(z + 2)

        @pl.when(z >= 2)
        def _():
            for copy in stores(z - 2, slot):
                copy.wait()

        scale = coefficient(kinds[z])
        one = first_out.at[slot].reshape(count * STEP, width)
        two = second_out.at[slot].reshape(count * STEP, width)
        for y in range(height):
            row = planes[z + 1, y + 1]
            beside = planes[z, y + 1] + planes[z + 2, y + 1]
            beside = beside + (planes[z + 1, y] + planes[z + 1, y + 2])
            beside = beside + beside_in_row(row, first, last)
            one[pl.ds(y, count, stride=STEP), :] = row
            two[pl.ds(y, count, stride=STEP), :] = scale[y : y + 1, :] * row - beside
        for copy in stores(z, slot):
            copy.start()
        return 0

    lax.fori_loop(0, depth, step, 0)
    for z in (depth - 2, depth - 1):
        for copy in stores(z, z % 2):
            copy.wait()


def device_sum(value):
    def shifted(axis, perm):
        return lax.ppermute(value, axis, perm)

    slabs = range(32)
    value = value + shifted("slab", [(i, i ^ 1) for i in slabs])
    for stride in (8, 2, 0):
        if stride:
            def move(i, d):
                place = (i // stride) % 4
                return i + ((place + d) % 4 - place) * stride
            axis, perms = "slab", [[(i, move(i, d)) for i in slabs] for d in (1, 2, 3)]
        else:
            axis = "pencil"
            perms = [[(i, (i + d) % 4) for i in range(4)] for d in (1, 2, 3)]
        left, opposite, right = [shifted(axis, perm) for perm in perms]
        value = (value + opposite) + (left + right)
    return value


def whole(memory=pltpu.VMEM):
    return pl.BlockSpec(memory_space=memory)


def local(basis, image, material, picked):
    columns, depth, height, width = basis.shape
    count = picked.shape[0]
    slabs, pencils = lax.axis_size("slab"), lax.axis_size("pencil")

    def neighbours(low_face, high_face, axis, size):
        up = [(i, i + 1) for i in range(size - 1)]
        down = [(j, i) for i, j in up]
        return lax.ppermute(high_face, axis, up), lax.ppermute(low_face, axis, down)

    face = jax.ShapeDtypeStruct((height, columns, width), BF16)
    edge = jax.ShapeDtypeStruct((depth, columns, width), BF16)
    turned, z_first, z_last, y_first, y_last = pl.pallas_call(
        turn_kernel,
        in_specs=[whole(pltpu.HBM)],
        out_specs=[whole()] * 5,
        out_shape=[jax.ShapeDtypeStruct((depth, height, columns, width), BF16), face, face, edge, edge],
        scratch_shapes=[
            pltpu.VMEM((3, columns, height, width), BF16),
            pltpu.SemaphoreType.DMA((3,)),
        ],
        compiler_params=pltpu.CompilerParams(vmem_limit_bytes=46 * MIB),
        name="turn",
    )(basis)
    z_low, z_high = neighbours(z_first, z_last, "slab", slabs)
    y_low, y_high = neighbours(y_first, y_last, "pencil", pencils)
    sums = pl.pallas_call(
        gram_kernel,
        in_specs=[whole(pltpu.SMEM), whole(pltpu.HBM), whole(pltpu.HBM)],
        out_specs=whole(),
        out_shape=jax.ShapeDtypeStruct((columns + count, columns), F32),
        scratch_shapes=[
            pltpu.VMEM((3, columns, height, width), BF16),
            pltpu.VMEM((count, depth, height, width), BF16),
            pltpu.VMEM(((columns + count) * PITCH, width), F32),
            pltpu.SemaphoreType.DMA((3,)),
            pltpu.SemaphoreType.DMA((count,)),
        ],
        compiler_params=pltpu.CompilerParams(vmem_limit_bytes=51 * MIB),
        cost_estimate=pl.CostEstimate(flops=2 * 10**9, bytes_accessed=17 * 10**6, transcendentals=0),
        name="gram",
    )(picked, image, basis)
    faces = (z_low, z_high, y_low, y_high)
    specs = [whole(), whole(pl.ANY), whole(pltpu.HBM), whole(pl.ANY), whole(pl.ANY), whole(), whole()]
    packed = pl.pallas_call(
        normal_kernel,
        in_specs=specs,
        out_specs=whole(),
        out_shape=jax.ShapeDtypeStruct((columns, 128), F32),
        scratch_shapes=[
            pltpu.VMEM((depth + 2, height, columns, width), BF16),
            pltpu.VMEM((depth, height, width), jnp.int32),
            pltpu.VMEM((2 * columns, columns), F32),
            pltpu.SemaphoreType.DMA((depth + 2,)),
            pltpu.SemaphoreType.DMA,
        ],
        compiler_params=pltpu.CompilerParams(vmem_limit_bytes=24 * MIB),
        name="normal",
    )(sums, turned, material, *faces)
    packed = device_sum(packed)
    grid_shape = (count, depth, height, width)
    return pl.pallas_call(
        update_kernel,
        in_specs=specs,
        out_specs=[whole(pltpu.HBM), whole(pltpu.HBM)],
        out_shape=[jax.ShapeDtypeStruct(grid_shape, F32)] * 2,
        scratch_shapes=[
            pltpu.VMEM((depth + 2, height, columns, width), BF16),
            pltpu.VMEM((depth, height, width), jnp.int32),
            pltpu.VMEM((depth + 2, height + 2, count, width), F32),
            pltpu.VMEM((2, count, STEP, width), F32),
            pltpu.VMEM((2, count, STEP, width), F32),
            pltpu.SemaphoreType.DMA((depth + 2,)),
            pltpu.SemaphoreType.DMA,
            pltpu.SemaphoreType.DMA((2, 2)),
        ],
        compiler_params=pltpu.CompilerParams(vmem_limit_bytes=32 * MIB),
        name="update",
    )(packed, turned, material, *faces)


def solution(mesh):
    field = P(None, "slab", "pencil", None)
    return jax.shard_map(
        local,
        mesh=mesh,
        in_specs=(field, field, P("slab", "pencil", None), P()),
        out_specs=(field, field),
        check_vma=False,
    )
```

```python
import jax
import jax.numpy as jnp
from jax import lax
from jax.experimental import pallas as pl
from jax.experimental.pallas import tpu as pltpu
from jax.sharding import PartitionSpec as P

F32 = jnp.float32
BF16 = jnp.bfloat16
CELLS = 4194304.0
PITCH = 44
STEP = 40
SLOTS = 2
NT = (((1,), (1,)), ((), ()))
TN = (((0,), (0,)), ((), ()))
MIB = 2**20


def turn_kernel(basis, turned, z_first, z_last, y_first, y_last, slab, sems):
    columns, depth, height, width = basis.shape
    slots = slab.shape[0]

    def load(z, slot):
        return pltpu.make_async_copy(basis.at[:, z], slab.at[slot], sems.at[slot])

    for z in range(slots - 1):
        load(z, z).start()

    def step(z, _):
        slot = lax.rem(z, slots)

        @pl.when(z + slots - 1 < depth)
        def _():
            load(z + slots - 1, lax.rem(z + slots - 1, slots)).start()

        load(z, slot).wait()
        for y in range(0, height, 16):
            part = jnp.swapaxes(slab[slot, :, y : y + 16, :], 0, 1)
            turned[z, y : y + 16] = part
            if y == 0:
                y_first[z] = part[0]
            if y + 16 == height:
                y_last[z] = part[15]
        return 0

    lax.fori_loop(0, depth, step, 0)
    z_first[...] = turned[0]
    z_last[...] = turned[depth - 1]


def gram_kernel(picked, image, basis, sums, image_slab, picked_slab, rows, sems, picked_sems):
    columns, depth, height, width = image.shape
    count = picked.shape[0]
    total = columns + count
    slots = image_slab.shape[0]

    def load(z, slot):
        return pltpu.make_async_copy(image.at[:, z], image_slab.at[slot], sems.at[slot])

    def load_picked(c):
        return pltpu.make_async_copy(basis.at[picked[c]], picked_slab.at[c], picked_sems.at[c])

    load(0, 0).start()
    for c in range(count):
        load_picked(c).start()
    for z in range(1, slots - 1):
        load(z, z).start()
    sums[...] = jnp.zeros_like(sums)
    for c in range(count):
        load_picked(c).wait()

    def step(z, _):
        slot = lax.rem(z, slots)

        @pl.when(z + slots - 1 < depth)
        def _():
            load(z + slots - 1, lax.rem(z + slots - 1, slots)).start()

        for c in range(count):
            at = (columns + c) * PITCH
            rows[at : at + height] = picked_slab[c, z].astype(F32)
        load(z, slot).wait()
        for c in range(columns):
            rows[c * PITCH : c * PITCH + height] = image_slab[slot, c].astype(F32)
        both = jnp.concatenate(
            [rows[pl.ds(y, total, stride=PITCH), :].astype(BF16) for y in range(height)], 1
        )
        sums[...] += lax.dot_general(both, both[:columns], NT, preferred_element_type=F32)
        return 0

    lax.fori_loop(0, depth, step, 0)


def coefficient(material):
    squared = jnp.where(
        material == 0, 0.3, jnp.where(material == 1, 0.9, jnp.where(material == 2, 1.6, 2.5))
    ).astype(F32)
    return 6.0 - squared


def beside_in_row(row, first, last):
    width = row.shape[1]
    up = jnp.where(first, 0.0, pltpu.roll(row, 1, 1))
    down = jnp.where(last, 0.0, pltpu.roll(row, width - 1, 1))
    return up + down


def normal_kernel(
    edges, sums, turned, material, z_low, z_high, y_low, y_high,
    packed, field, kinds, gram, sems, kind_sem,
):
    depth, height, columns, width = turned.shape
    count = sums.shape[0] - columns
    kind_load = pltpu.make_async_copy(material, kinds, kind_sem)
    loads = [pltpu.make_async_copy(z_low, field.at[0], sems.at[0])]
    for z in range(depth):
        loads.append(pltpu.make_async_copy(turned.at[z], field.at[z + 1], sems.at[z + 1]))
    loads.append(pltpu.make_async_copy(z_high, field.at[depth + 1], sems.at[depth + 1]))
    for copy in [kind_load] + loads:
        copy.start()
    gram[...] = jnp.zeros_like(gram)
    lane = lax.broadcasted_iota(jnp.int32, (columns, width), 1)
    first, last = lane == 0, lane == width - 1
    kind_load.wait()
    loads[0].wait()
    loads[1].wait()

    @pl.when(edges[0] == 0)
    def _():
        field[0] = jnp.zeros(field.shape[1:], BF16)

    inside = [edges[i].astype(F32) for i in (2, 3)]

    def step(z, _):
        @pl.when(z < depth - 1)
        def _():
            pltpu.make_async_copy(turned.at[z + 1], field.at[z + 2], sems.at[z + 2]).wait()

        @pl.when(z == depth - 1)
        def _():
            loads[depth + 1].wait()

            @pl.when(edges[1] == 0)
            def _():
                field[depth + 1] = jnp.zeros(field.shape[1:], BF16)

        scale = coefficient(kinds[z])
        middle = [y_low[z].astype(F32) * inside[0], field[z + 1, 0].astype(F32)]
        highs, lows = [], []
        for y in range(height):
            if y == height - 1:
                middle.append(y_high[z].astype(F32) * inside[1])
            else:
                middle.append(field[z + 1, y + 1].astype(F32))
            row = middle[y + 1]
            beside = field[z, y].astype(F32) + field[z + 2, y].astype(F32)
            beside = beside + (middle[y] + middle[y + 2])
            beside = beside + beside_in_row(row, first, last)
            image = scale[y : y + 1, :] * row - beside
            rounded = image.astype(BF16)
            highs.append(rounded)
            lows.append((image - rounded.astype(F32)).astype(BF16))
        rounded = jnp.concatenate(highs, 1)
        gap = jnp.zeros((16 - columns % 16, height * width), BF16)
        both = jnp.concatenate([rounded, gap, jnp.concatenate(lows, 1)], 0)
        part = lax.dot_general(both, rounded, NT, preferred_element_type=F32)
        gram[:columns] += part[:columns]
        gram[columns:] += part[both.shape[0] - columns :]
        return 0

    lax.fori_loop(0, depth, step, 0)
    side = jnp.zeros((columns, 128 - columns), F32)
    foot = jnp.zeros((128 - columns, 128), F32)
    cross = jnp.concatenate([gram[columns:], side], 1)
    cross_t = jnp.concatenate([cross, foot], 0).T[:columns]
    normal = jnp.concatenate([gram[:columns], side], 1) + cross + cross_t
    col = lax.broadcasted_iota(jnp.int32, (columns, 128), 1)
    line = lax.broadcasted_iota(jnp.int32, (columns, 128), 0)
    diagonal = jnp.sum(jnp.where(line == col, normal, 0.0), axis=1, keepdims=True)
    grams = sums[:columns]
    picked_t = jnp.concatenate(
        [jnp.concatenate([sums[columns:], jnp.zeros((count, 128 - columns), F32)], 1),
         jnp.zeros((128 - count, 128), F32)], 0
    ).T[:columns]
    placed = pltpu.roll(picked_t, columns, 1)
    grams = jnp.concatenate([grams, side], 1)
    out = jnp.where(line >= col, grams, normal)
    out = jnp.where(col >= columns, placed, out)
    packed[...] = jnp.where(col == columns + count, diagonal, out)


def spread(row, lane):
    return jnp.broadcast_to(row[:, lane : lane + 1], row.shape)


def eliminate(blocks, panel, followers):
    base = 8 * panel
    wide = blocks[panel].shape
    rows = [jnp.broadcast_to(blocks[panel][i : i + 1, :], wide) for i in range(8)]
    heads = [[spread(rows[i], base + j) for j in range(8)] for i in range(8)]
    forward, pivots = [], []
    for k in range(8):
        forward.append(rows[k])
        pivots.append(heads[k][k])
        inverse = 1.0 / heads[k][k]
        rows[k] = rows[k] * inverse
        for j in range(k + 1, 8):
            heads[k][j] = heads[k][j] * inverse
        for i in range(8):
            if i == k:
                continue
            factor = heads[i][k]
            rows[i] = rows[i] - factor * rows[k]
            for j in range(k + 1, 8):
                heads[i][j] = heads[i][j] - factor * heads[k][j]
    for i in followers:
        block = blocks[i]
        for j in range(8):
            block = block - spread(blocks[i], base + j) * rows[j]
        blocks[i] = block
    return rows, forward, pivots


def stacked(rows):
    line = lax.broadcasted_iota(jnp.int32, rows[0].shape, 0)
    out = rows[0]
    for i in range(1, 8):
        out = jnp.where(line == i, rows[i], out)
    return out


def combination(packed, columns, count):
    exact = lax.Precision.HIGHEST
    shape = (128, 128)
    col = lax.broadcasted_iota(jnp.int32, shape, 1)
    line = lax.broadcasted_iota(jnp.int32, shape, 0)
    full = jnp.concatenate([packed, jnp.zeros((128 - columns, 128), F32)], 0)
    flipped = full.T
    grams = jnp.where(line >= col, full, flipped)
    grams = jnp.where(col >= columns, full, grams)
    diagonal = jnp.broadcast_to(full[:, columns + count : columns + count + 1], shape)
    normal = jnp.where(line < col, full, flipped)
    normal = jnp.where(line == col, diagonal, normal)
    normal = jnp.where((col < columns) & (line < columns), normal, 0.0)
    blocks = [grams[8 * i : 8 * i + 8] for i in range(columns // 8)]
    for panel in range(len(blocks)):
        rest = [i for i in range(len(blocks)) if i != panel]
        rows, _, _ = eliminate(blocks, panel, rest)
        blocks[panel] = stacked(rows)
    solved = jnp.concatenate(blocks + [jnp.zeros((128 - columns, 128), F32)], 0)
    solved = pltpu.roll(solved, 128 - columns, 1)
    chosen = jnp.where(col < count, solved, 0.0).astype(BF16).astype(F32)
    chosen_t = chosen.T
    product = jnp.dot(normal, chosen, precision=exact, preferred_element_type=F32)
    normal = jnp.dot(chosen_t, product, precision=exact, preferred_element_type=F32)
    normal = normal[:count] * (1.0 / CELLS)
    joined = jnp.where(col[:count] < count, normal, pltpu.roll(chosen_t[:count], count, 1))
    blocks = [joined[8 * i : 8 * i + 8] for i in range(count // 8)]
    for panel in range(len(blocks)):
        rest = range(panel + 1, len(blocks))
        _, forward, pivots = eliminate(blocks, panel, rest)
        blocks[panel] = stacked([r * lax.rsqrt(d) for r, d in zip(forward, pivots)])
    return pltpu.roll(jnp.concatenate(blocks, 0), 128 - count, 1)[:, :columns]


def update_kernel(
    edges, packed, turned, material, z_low, z_high, y_low, y_high, recycle, images,
    field, kinds, planes, first_out, second_out, load_sems, kind_sem, store_sems,
):
    depth, height, columns, width = turned.shape
    count = recycle.shape[0]
    loads = [pltpu.make_async_copy(z_low, field.at[0], load_sems.at[0])]
    for z in range(depth):
        loads.append(pltpu.make_async_copy(turned.at[z], field.at[z + 1], load_sems.at[z + 1]))
    loads.append(pltpu.make_async_copy(z_high, field.at[depth + 1], load_sems.at[depth + 1]))
    loads.append(pltpu.make_async_copy(material, kinds, kind_sem))
    for copy in loads:
        copy.start()
    weights = combination(packed[...], columns, count)
    rounded = weights.astype(BF16)
    both = jnp.concatenate([rounded, (weights - rounded.astype(F32)).astype(BF16)], 0)

    def combine(row):
        part = jnp.dot(both, row, preferred_element_type=F32)
        return part[:count] + part[count:]

    low = combine(jnp.concatenate([y_low[z] for z in range(depth)], 1))
    high = combine(jnp.concatenate([y_high[z] for z in range(depth)], 1))
    for z in range(depth):
        planes[z + 1, 0] = low[:, z * width : (z + 1) * width] * edges[2].astype(F32)
        planes[z + 1, height + 1] = high[:, z * width : (z + 1) * width] * edges[3].astype(F32)
    for copy in loads:
        copy.wait()

    @pl.when(edges[0] == 0)
    def _():
        field[0] = jnp.zeros(field.shape[1:], BF16)

    @pl.when(edges[1] == 0)
    def _():
        field[depth + 1] = jnp.zeros(field.shape[1:], BF16)

    def fill(z):
        plane = combine(jnp.concatenate([field[z, y] for y in range(height)], 1))
        for y in range(height):
            planes[z, y + 1] = plane[:, y * width : (y + 1) * width]

    def stores(z, slot):
        return (
            pltpu.make_async_copy(first_out.at[slot, :, :height], recycle.at[:, z], store_sems.at[slot, 0]),
            pltpu.make_async_copy(second_out.at[slot, :, :height], images.at[:, z], store_sems.at[slot, 1]),
        )

    fill(0)
    fill(1)
    lane = lax.broadcasted_iota(jnp.int32, (count, width), 1)
    first, last = lane == 0, lane == width - 1

    def step(z, _):
        slot = lax.rem(z, SLOTS)
        fill(z + 2)

        @pl.when(z >= SLOTS)
        def _():
            for copy in stores(z - SLOTS, slot):
                copy.wait()

        scale = coefficient(kinds[z])
        one = first_out.at[slot].reshape(count * STEP, width)
        two = second_out.at[slot].reshape(count * STEP, width)
        for y in range(height):
            row = planes[z + 1, y + 1]
            beside = planes[z, y + 1] + planes[z + 2, y + 1]
            beside = beside + (planes[z + 1, y] + planes[z + 1, y + 2])
            beside = beside + beside_in_row(row, first, last)
            one[pl.ds(y, count, stride=STEP), :] = row
            two[pl.ds(y, count, stride=STEP), :] = scale[y : y + 1, :] * row - beside
        for copy in stores(z, slot):
            copy.start()
        return 0

    lax.fori_loop(0, depth, step, 0)
    for z in range(depth - SLOTS, depth):
        for copy in stores(z, z % SLOTS):
            copy.wait()


def device_sum(value):
    def shifted(axis, perm):
        return lax.ppermute(value, axis, perm)

    slabs = range(32)
    value = value + shifted("slab", [(i, i ^ 1) for i in slabs])
    for stride in (8, 2, 0):
        if stride:
            def move(i, d):
                place = (i // stride) % 4
                return i + ((place + d) % 4 - place) * stride
            axis, perms = "slab", [[(i, move(i, d)) for i in slabs] for d in (1, 2, 3)]
        else:
            axis = "pencil"
            perms = [[(i, (i + d) % 4) for i in range(4)] for d in (1, 2, 3)]
        left, opposite, right = [shifted(axis, perm) for perm in perms]
        value = (value + opposite) + (left + right)
    return value


def whole(memory=pltpu.VMEM):
    return pl.BlockSpec(memory_space=memory)


def local(basis, image, material, picked):
    columns, depth, height, width = basis.shape
    count = picked.shape[0]
    slabs, pencils = lax.axis_size("slab"), lax.axis_size("pencil")

    def neighbours(low_face, high_face, axis, size):
        up = [(i, (i + 1) % size) for i in range(size)]
        down = [(j, i) for i, j in up]
        return lax.ppermute(high_face, axis, up), lax.ppermute(low_face, axis, down)

    face = jax.ShapeDtypeStruct((height, columns, width), BF16)
    edge = jax.ShapeDtypeStruct((depth, columns, width), BF16)
    turned, z_first, z_last, y_first, y_last = pl.pallas_call(
        turn_kernel,
        in_specs=[whole(pltpu.HBM)],
        out_specs=[whole()] * 5,
        out_shape=[jax.ShapeDtypeStruct((depth, height, columns, width), BF16), face, face, edge, edge],
        scratch_shapes=[
            pltpu.VMEM((3, columns, height, width), BF16),
            pltpu.SemaphoreType.DMA((3,)),
        ],
        compiler_params=pltpu.CompilerParams(vmem_limit_bytes=46 * MIB),
        name="turn",
    )(basis)
    z_low, z_high = neighbours(z_first, z_last, "slab", slabs)
    y_low, y_high = neighbours(y_first, y_last, "pencil", pencils)
    sums = pl.pallas_call(
        gram_kernel,
        in_specs=[whole(pltpu.SMEM), whole(pltpu.HBM), whole(pltpu.HBM)],
        out_specs=whole(),
        out_shape=jax.ShapeDtypeStruct((columns + count, columns), F32),
        scratch_shapes=[
            pltpu.VMEM((3, columns, height, width), BF16),
            pltpu.VMEM((count, depth, height, width), BF16),
            pltpu.VMEM(((columns + count) * PITCH, width), F32),
            pltpu.SemaphoreType.DMA((3,)),
            pltpu.SemaphoreType.DMA((count,)),
        ],
        compiler_params=pltpu.CompilerParams(vmem_limit_bytes=51 * MIB),
        cost_estimate=pl.CostEstimate(flops=2 * 10**9, bytes_accessed=17 * 10**6, transcendentals=0),
        name="gram",
    )(picked, image, basis)
    faces = (z_low, z_high, y_low, y_high)
    slab, pencil = lax.axis_index("slab"), lax.axis_index("pencil")
    inner = (slab > 0, slab < slabs - 1, pencil > 0, pencil < pencils - 1)
    edges = jnp.stack(inner).astype(jnp.int32)
    specs = [whole(pltpu.SMEM), whole(), whole(pl.ANY), whole(pltpu.HBM), whole(pl.ANY), whole(pl.ANY), whole(), whole()]
    packed = pl.pallas_call(
        normal_kernel,
        in_specs=specs,
        out_specs=whole(),
        out_shape=jax.ShapeDtypeStruct((columns, 128), F32),
        scratch_shapes=[
            pltpu.VMEM((depth + 2, height, columns, width), BF16),
            pltpu.VMEM((depth, height, width), jnp.int32),
            pltpu.VMEM((2 * columns, columns), F32),
            pltpu.SemaphoreType.DMA((depth + 2,)),
            pltpu.SemaphoreType.DMA,
        ],
        compiler_params=pltpu.CompilerParams(vmem_limit_bytes=24 * MIB),
        name="normal",
    )(edges, sums, turned, material, *faces)
    packed = device_sum(packed)
    grid_shape = (count, depth, height, width)
    return pl.pallas_call(
        update_kernel,
        in_specs=specs,
        out_specs=[whole(pltpu.HBM), whole(pltpu.HBM)],
        out_shape=[jax.ShapeDtypeStruct(grid_shape, F32)] * 2,
        scratch_shapes=[
            pltpu.VMEM((depth + 2, height, columns, width), BF16),
            pltpu.VMEM((depth, height, width), jnp.int32),
            pltpu.VMEM((depth + 2, height + 2, count, width), F32),
            pltpu.VMEM((SLOTS, count, STEP, width), F32),
            pltpu.VMEM((SLOTS, count, STEP, width), F32),
            pltpu.SemaphoreType.DMA((depth + 2,)),
            pltpu.SemaphoreType.DMA,
            pltpu.SemaphoreType.DMA((SLOTS, 2)),
        ],
        compiler_params=pltpu.CompilerParams(vmem_limit_bytes=32 * MIB),
        name="update",
    )(edges, packed, turned, material, *faces)


def solution(mesh):
    field = P(None, "slab", "pencil", None)
    return jax.shard_map(
        local,
        mesh=mesh,
        in_specs=(field, field, P("slab", "pencil", None), P()),
        out_specs=(field, field),
        check_vma=False,
    )
```

```python
import jax
import jax.numpy as jnp
from jax import lax
from jax.experimental import pallas as pl
from jax.experimental.pallas import tpu as pltpu
from jax.sharding import PartitionSpec as P

F32 = jnp.float32
BF16 = jnp.bfloat16
CELLS = 4194304.0
PITCH = 44
STEP = 40
SLOTS = 2
NT = (((1,), (1,)), ((), ()))
TN = (((0,), (0,)), ((), ()))
MIB = 2**20


def turn_kernel(basis, turned, z_first, z_last, y_first, y_last, slab, sems):
    columns, depth, height, width = basis.shape
    slots = slab.shape[0]

    def load(z, slot):
        return pltpu.make_async_copy(basis.at[:, z], slab.at[slot], sems.at[slot])

    for z in range(slots - 1):
        load(z, z).start()

    def step(z, _):
        slot = lax.rem(z, slots)

        @pl.when(z + slots - 1 < depth)
        def _():
            load(z + slots - 1, lax.rem(z + slots - 1, slots)).start()

        load(z, slot).wait()
        for y in range(0, height, 16):
            part = jnp.swapaxes(slab[slot, :, y : y + 16, :], 0, 1)
            turned[z, y : y + 16] = part
            if y == 0:
                y_first[z] = part[0]
            if y + 16 == height:
                y_last[z] = part[15]
        return 0

    lax.fori_loop(0, depth, step, 0)
    z_first[...] = turned[0]
    z_last[...] = turned[depth - 1]


def gram_kernel(picked, image, basis, sums, image_slab, picked_slab, rows, sems, picked_sems):
    columns, depth, height, width = image.shape
    count = picked.shape[0]
    total = columns + count
    slots = image_slab.shape[0]

    def load(z, slot):
        return pltpu.make_async_copy(image.at[:, z], image_slab.at[slot], sems.at[slot])

    def load_picked(c):
        return pltpu.make_async_copy(basis.at[picked[c]], picked_slab.at[c], picked_sems.at[c])

    load(0, 0).start()
    for c in range(count):
        load_picked(c).start()
    for z in range(1, slots - 1):
        load(z, z).start()
    sums[...] = jnp.zeros_like(sums)
    for c in range(count):
        load_picked(c).wait()

    def step(z, _):
        slot = lax.rem(z, slots)

        @pl.when(z + slots - 1 < depth)
        def _():
            load(z + slots - 1, lax.rem(z + slots - 1, slots)).start()

        for c in range(count):
            at = (columns + c) * PITCH
            rows[at : at + height] = picked_slab[c, z].astype(F32)
        load(z, slot).wait()
        for c in range(columns):
            rows[c * PITCH : c * PITCH + height] = image_slab[slot, c].astype(F32)
        both = jnp.concatenate(
            [rows[pl.ds(y, total, stride=PITCH), :].astype(BF16) for y in range(height)], 1
        )
        sums[...] += lax.dot_general(both, both[:columns], NT, preferred_element_type=F32)
        return 0

    lax.fori_loop(0, depth, step, 0)


def coefficient(material):
    squared = jnp.where(
        material == 0, 0.3, jnp.where(material == 1, 0.9, jnp.where(material == 2, 1.6, 2.5))
    ).astype(F32)
    return 6.0 - squared


def beside_in_row(row, first, last):
    width = row.shape[1]
    up = jnp.where(first, 0.0, pltpu.roll(row, 1, 1))
    down = jnp.where(last, 0.0, pltpu.roll(row, width - 1, 1))
    return up + down


def normal_kernel(
    edges, sums, turned, material, z_low, z_high, y_low, y_high,
    packed, field, kinds, gram, sems, kind_sem,
):
    depth, height, columns, width = turned.shape
    count = sums.shape[0] - columns
    kind_load = pltpu.make_async_copy(material, kinds, kind_sem)
    loads = [pltpu.make_async_copy(z_low, field.at[0], sems.at[0])]
    for z in range(depth):
        loads.append(pltpu.make_async_copy(turned.at[z], field.at[z + 1], sems.at[z + 1]))
    loads.append(pltpu.make_async_copy(z_high, field.at[depth + 1], sems.at[depth + 1]))
    for copy in [kind_load] + loads[:4]:
        copy.start()
    gram[...] = jnp.zeros_like(gram)
    lane = lax.broadcasted_iota(jnp.int32, (columns, width), 1)
    first, last = lane == 0, lane == width - 1
    kind_load.wait()
    loads[0].wait()
    loads[1].wait()

    @pl.when(edges[0] == 0)
    def _():
        field[0] = jnp.zeros(field.shape[1:], BF16)

    inside = [edges[i].astype(F32) for i in (2, 3)]

    def step(z, _):
        @pl.when(z + 3 < depth)
        def _():
            pltpu.make_async_copy(turned.at[z + 3], field.at[z + 4], sems.at[z + 4]).start()

        @pl.when(z + 3 == depth)
        def _():
            loads[depth + 1].start()

        @pl.when(z < depth - 1)
        def _():
            pltpu.make_async_copy(turned.at[z + 1], field.at[z + 2], sems.at[z + 2]).wait()

        @pl.when(z == depth - 1)
        def _():
            loads[depth + 1].wait()

            @pl.when(edges[1] == 0)
            def _():
                field[depth + 1] = jnp.zeros(field.shape[1:], BF16)

        scale = coefficient(kinds[z])
        middle = [y_low[z].astype(F32) * inside[0], field[z + 1, 0].astype(F32)]
        highs, lows = [], []
        for y in range(height):
            if y == height - 1:
                middle.append(y_high[z].astype(F32) * inside[1])
            else:
                middle.append(field[z + 1, y + 1].astype(F32))
            row = middle[y + 1]
            beside = field[z, y].astype(F32) + field[z + 2, y].astype(F32)
            beside = beside + (middle[y] + middle[y + 2])
            beside = beside + beside_in_row(row, first, last)
            image = scale[y : y + 1, :] * row - beside
            rounded = image.astype(BF16)
            highs.append(rounded)
            lows.append((image - rounded.astype(F32)).astype(BF16))
        rounded = jnp.concatenate(highs, 1)
        gap = jnp.zeros((16 - columns % 16, height * width), BF16)
        both = jnp.concatenate([rounded, gap, jnp.concatenate(lows, 1)], 0)
        part = lax.dot_general(both, rounded, NT, preferred_element_type=F32)
        gram[:columns] += part[:columns]
        gram[columns:] += part[both.shape[0] - columns :]
        return 0

    lax.fori_loop(0, depth, step, 0)
    side = jnp.zeros((columns, 128 - columns), F32)
    foot = jnp.zeros((128 - columns, 128), F32)
    cross = jnp.concatenate([gram[columns:], side], 1)
    cross_t = jnp.concatenate([cross, foot], 0).T[:columns]
    normal = jnp.concatenate([gram[:columns], side], 1) + cross + cross_t
    col = lax.broadcasted_iota(jnp.int32, (columns, 128), 1)
    line = lax.broadcasted_iota(jnp.int32, (columns, 128), 0)
    diagonal = jnp.sum(jnp.where(line == col, normal, 0.0), axis=1, keepdims=True)
    grams = sums[:columns]
    picked_t = jnp.concatenate(
        [jnp.concatenate([sums[columns:], jnp.zeros((count, 128 - columns), F32)], 1),
         jnp.zeros((128 - count, 128), F32)], 0
    ).T[:columns]
    placed = pltpu.roll(picked_t, columns, 1)
    grams = jnp.concatenate([grams, side], 1)
    out = jnp.where(line >= col, grams, normal)
    out = jnp.where(col >= columns, placed, out)
    packed[...] = jnp.where(col == columns + count, diagonal, out)


def spread(row, lane):
    return jnp.broadcast_to(row[:, lane : lane + 1], row.shape)


def eliminate(blocks, panel, followers):
    base = 8 * panel
    wide = blocks[panel].shape
    rows = [jnp.broadcast_to(blocks[panel][i : i + 1, :], wide) for i in range(8)]
    heads = [[spread(rows[i], base + j) for j in range(8)] for i in range(8)]
    forward, pivots = [], []
    for k in range(8):
        forward.append(rows[k])
        pivots.append(heads[k][k])
        inverse = 1.0 / heads[k][k]
        rows[k] = rows[k] * inverse
        for j in range(k + 1, 8):
            heads[k][j] = heads[k][j] * inverse
        for i in range(8):
            if i == k:
                continue
            factor = heads[i][k]
            rows[i] = rows[i] - factor * rows[k]
            for j in range(k + 1, 8):
                heads[i][j] = heads[i][j] - factor * heads[k][j]
    for i in followers:
        block = blocks[i]
        for j in range(8):
            block = block - spread(blocks[i], base + j) * rows[j]
        blocks[i] = block
    return rows, forward, pivots


def stacked(rows):
    line = lax.broadcasted_iota(jnp.int32, rows[0].shape, 0)
    out = rows[0]
    for i in range(1, 8):
        out = jnp.where(line == i, rows[i], out)
    return out


def combination(packed, columns, count):
    exact = lax.Precision.HIGHEST
    shape = (128, 128)
    col = lax.broadcasted_iota(jnp.int32, shape, 1)
    line = lax.broadcasted_iota(jnp.int32, shape, 0)
    full = jnp.concatenate([packed, jnp.zeros((128 - columns, 128), F32)], 0)
    flipped = full.T
    grams = jnp.where(line >= col, full, flipped)
    grams = jnp.where(col >= columns, full, grams)
    diagonal = jnp.broadcast_to(full[:, columns + count : columns + count + 1], shape)
    normal = jnp.where(line < col, full, flipped)
    normal = jnp.where(line == col, diagonal, normal)
    normal = jnp.where((col < columns) & (line < columns), normal, 0.0)
    blocks = [grams[8 * i : 8 * i + 8] for i in range(columns // 8)]
    for panel in range(len(blocks)):
        rest = [i for i in range(len(blocks)) if i != panel]
        rows, _, _ = eliminate(blocks, panel, rest)
        blocks[panel] = stacked(rows)
    solved = jnp.concatenate(blocks + [jnp.zeros((128 - columns, 128), F32)], 0)
    solved = pltpu.roll(solved, 128 - columns, 1)
    chosen = jnp.where(col < count, solved, 0.0).astype(BF16).astype(F32)
    chosen_t = chosen.T
    product = jnp.dot(normal, chosen, precision=exact, preferred_element_type=F32)
    normal = jnp.dot(chosen_t, product, precision=exact, preferred_element_type=F32)
    normal = normal[:count] * (1.0 / CELLS)
    joined = jnp.where(col[:count] < count, normal, pltpu.roll(chosen_t[:count], count, 1))
    blocks = [joined[8 * i : 8 * i + 8] for i in range(count // 8)]
    for panel in range(len(blocks)):
        rest = range(panel + 1, len(blocks))
        _, forward, pivots = eliminate(blocks, panel, rest)
        blocks[panel] = stacked([r * lax.rsqrt(d) for r, d in zip(forward, pivots)])
    return pltpu.roll(jnp.concatenate(blocks, 0), 128 - count, 1)[:, :columns]


def update_kernel(
    edges, packed, turned, material, z_low, z_high, y_low, y_high, recycle, images,
    planes, first_out, second_out, store_sems,
):
    depth, height, columns, width = turned.shape
    count = recycle.shape[0]
    weights = combination(packed[...], columns, count)
    rounded = weights.astype(BF16)
    both = jnp.concatenate([rounded, (weights - rounded.astype(F32)).astype(BF16)], 0)

    def combine(row):
        part = jnp.dot(both, row, preferred_element_type=F32)
        return part[:count] + part[count:]

    low = combine(jnp.concatenate([y_low[z] for z in range(depth)], 1))
    high = combine(jnp.concatenate([y_high[z] for z in range(depth)], 1))
    for z in range(depth):
        planes[z + 1, 0] = low[:, z * width : (z + 1) * width] * edges[2].astype(F32)
        planes[z + 1, height + 1] = high[:, z * width : (z + 1) * width] * edges[3].astype(F32)

    def fill(z, source, keep=None):
        plane = combine(jnp.concatenate([source[y] for y in range(height)], 1))
        if keep is not None:
            plane = plane * keep.astype(F32)
        for y in range(height):
            planes[z, y + 1] = plane[:, y * width : (y + 1) * width]

    def stores(z, slot):
        return (
            pltpu.make_async_copy(first_out.at[slot, :, :height], recycle.at[:, z], store_sems.at[slot, 0]),
            pltpu.make_async_copy(second_out.at[slot, :, :height], images.at[:, z], store_sems.at[slot, 1]),
        )

    fill(0, z_low, edges[0])
    fill(1, turned.at[0])
    fill(depth + 1, z_high, edges[1])
    lane = lax.broadcasted_iota(jnp.int32, (count, width), 1)
    first, last = lane == 0, lane == width - 1

    def step(z, _):
        slot = lax.rem(z, SLOTS)

        @pl.when(z + 1 < depth)
        def _():
            fill(z + 2, turned.at[z + 1])

        @pl.when(z >= SLOTS)
        def _():
            for copy in stores(z - SLOTS, slot):
                copy.wait()

        scale = coefficient(material[z])
        one = first_out.at[slot].reshape(count * STEP, width)
        two = second_out.at[slot].reshape(count * STEP, width)
        for y in range(height):
            row = planes[z + 1, y + 1]
            beside = planes[z, y + 1] + planes[z + 2, y + 1]
            beside = beside + (planes[z + 1, y] + planes[z + 1, y + 2])
            beside = beside + beside_in_row(row, first, last)
            one[pl.ds(y, count, stride=STEP), :] = row
            two[pl.ds(y, count, stride=STEP), :] = scale[y : y + 1, :] * row - beside
        for copy in stores(z, slot):
            copy.start()
        return 0

    lax.fori_loop(0, depth, step, 0)
    for z in range(depth - SLOTS, depth):
        for copy in stores(z, z % SLOTS):
            copy.wait()


def device_sum(value):
    def shifted(axis, perm):
        return lax.ppermute(value, axis, perm)

    slabs = range(32)
    value = value + shifted("slab", [(i, i ^ 1) for i in slabs])
    for stride in (8, 2, 0):
        if stride:
            def move(i, d):
                place = (i // stride) % 4
                return i + ((place + d) % 4 - place) * stride
            axis, perms = "slab", [[(i, move(i, d)) for i in slabs] for d in (1, 2, 3)]
        else:
            axis = "pencil"
            perms = [[(i, (i + d) % 4) for i in range(4)] for d in (1, 2, 3)]
        left, opposite, right = [shifted(axis, perm) for perm in perms]
        value = (value + opposite) + (left + right)
    return value


def whole(memory=pltpu.VMEM):
    return pl.BlockSpec(memory_space=memory)


def local(basis, image, material, picked):
    columns, depth, height, width = basis.shape
    count = picked.shape[0]
    slabs, pencils = lax.axis_size("slab"), lax.axis_size("pencil")

    def neighbours(low_face, high_face, axis, size):
        up = [(i, (i + 1) % size) for i in range(size)]
        down = [(j, i) for i, j in up]
        return lax.ppermute(high_face, axis, up), lax.ppermute(low_face, axis, down)

    face = jax.ShapeDtypeStruct((height, columns, width), BF16)
    edge = jax.ShapeDtypeStruct((depth, columns, width), BF16)
    turned, z_first, z_last, y_first, y_last = pl.pallas_call(
        turn_kernel,
        in_specs=[whole(pltpu.HBM)],
        out_specs=[whole()] * 5,
        out_shape=[jax.ShapeDtypeStruct((depth, height, columns, width), BF16), face, face, edge, edge],
        scratch_shapes=[
            pltpu.VMEM((3, columns, height, width), BF16),
            pltpu.SemaphoreType.DMA((3,)),
        ],
        compiler_params=pltpu.CompilerParams(vmem_limit_bytes=46 * MIB),
        name="turn",
    )(basis)
    z_low, z_high = neighbours(z_first, z_last, "slab", slabs)
    y_low, y_high = neighbours(y_first, y_last, "pencil", pencils)
    sums = pl.pallas_call(
        gram_kernel,
        in_specs=[whole(pltpu.SMEM), whole(pltpu.HBM), whole(pltpu.HBM)],
        out_specs=whole(),
        out_shape=jax.ShapeDtypeStruct((columns + count, columns), F32),
        scratch_shapes=[
            pltpu.VMEM((3, columns, height, width), BF16),
            pltpu.VMEM((count, depth, height, width), BF16),
            pltpu.VMEM(((columns + count) * PITCH, width), F32),
            pltpu.SemaphoreType.DMA((3,)),
            pltpu.SemaphoreType.DMA((count,)),
        ],
        compiler_params=pltpu.CompilerParams(vmem_limit_bytes=49 * MIB),
        cost_estimate=pl.CostEstimate(flops=2 * 10**9, bytes_accessed=17 * 10**6, transcendentals=0),
        name="gram",
    )(picked, image, basis)
    faces = (z_low, z_high, y_low, y_high)
    slab, pencil = lax.axis_index("slab"), lax.axis_index("pencil")
    inner = (slab > 0, slab < slabs - 1, pencil > 0, pencil < pencils - 1)
    edges = jnp.stack(inner).astype(jnp.int32)
    specs = [whole(pltpu.SMEM), whole(), whole(pl.ANY), whole(pltpu.HBM), whole(pl.ANY), whole(pl.ANY), whole(), whole()]
    packed = pl.pallas_call(
        normal_kernel,
        in_specs=specs,
        out_specs=whole(),
        out_shape=jax.ShapeDtypeStruct((columns, 128), F32),
        scratch_shapes=[
            pltpu.VMEM((depth + 2, height, columns, width), BF16),
            pltpu.VMEM((depth, height, width), jnp.int32),
            pltpu.VMEM((2 * columns, columns), F32),
            pltpu.SemaphoreType.DMA((depth + 2,)),
            pltpu.SemaphoreType.DMA,
        ],
        compiler_params=pltpu.CompilerParams(vmem_limit_bytes=24 * MIB),
        name="normal",
    )(edges, sums, turned, material, *faces)
    packed = device_sum(packed)
    grid_shape = (count, depth, height, width)
    return pl.pallas_call(
        update_kernel,
        in_specs=[whole(pltpu.SMEM)] + [whole()] * 7,
        out_specs=[whole(pltpu.HBM), whole(pltpu.HBM)],
        out_shape=[jax.ShapeDtypeStruct(grid_shape, F32)] * 2,
        scratch_shapes=[
            pltpu.VMEM((depth + 2, height + 2, count, width), F32),
            pltpu.VMEM((SLOTS, count, STEP, width), F32),
            pltpu.VMEM((SLOTS, count, STEP, width), F32),
            pltpu.SemaphoreType.DMA((SLOTS, 2)),
        ],
        compiler_params=pltpu.CompilerParams(vmem_limit_bytes=20 * MIB),
        name="update",
    )(edges, packed, turned, material, *faces)


def solution(mesh):
    field = P(None, "slab", "pencil", None)
    return jax.shard_map(
        local,
        mesh=mesh,
        in_specs=(field, field, P("slab", "pencil", None), P()),
        out_specs=(field, field),
        check_vma=False,
    )
```

```python
import jax
import jax.numpy as jnp
from jax import lax
from jax.experimental import pallas as pl
from jax.experimental.pallas import tpu as pltpu
from jax.sharding import PartitionSpec as P

F32 = jnp.float32
BF16 = jnp.bfloat16
CELLS = 4194304.0
PITCH = 44
STEP = 40
SLOTS = 2
NT = (((1,), (1,)), ((), ()))
TN = (((0,), (0,)), ((), ()))
MIB = 2**20


def turn_kernel(basis, turned, z_first, z_last, y_first, y_last, slab, moved, sems, out_sems):
    columns, depth, height, width = basis.shape
    slots = slab.shape[0]

    def load(z, slot):
        return pltpu.make_async_copy(basis.at[:, z], slab.at[slot], sems.at[slot])

    def store(z, slot):
        return pltpu.make_async_copy(moved.at[slot], turned.at[z], out_sems.at[slot])

    for z in range(slots - 1):
        load(z, z).start()

    def step(z, _):
        slot = lax.rem(z, slots)

        @pl.when(z + slots - 1 < depth)
        def _():
            load(z + slots - 1, lax.rem(z + slots - 1, slots)).start()

        @pl.when(z >= slots)
        def _():
            store(z - slots, slot).wait()

        load(z, slot).wait()
        for y in range(0, height, 16):
            part = jnp.swapaxes(slab[slot, :, y : y + 16, :], 0, 1)
            moved[slot, y : y + 16] = part
            if y == 0:
                y_first[z] = part[0]
            if y + 16 == height:
                y_last[z] = part[15]
        store(z, slot).start()

        @pl.when(z == 0)
        def _():
            z_first[...] = moved[0]

        return 0

    lax.fori_loop(0, depth, step, 0)
    z_last[...] = moved[(depth - 1) % slots]
    for z in range(depth - slots, depth):
        store(z, z % slots).wait()


def gram_kernel(picked, image, basis, sums, image_slab, picked_slab, rows, sems, picked_sems):
    columns, depth, height, width = image.shape
    count = picked.shape[0]
    total = columns + count
    slots = image_slab.shape[0]

    def load(z, slot):
        return pltpu.make_async_copy(image.at[:, z], image_slab.at[slot], sems.at[slot])

    def load_picked(c):
        return pltpu.make_async_copy(basis.at[picked[c]], picked_slab.at[c], picked_sems.at[c])

    load(0, 0).start()
    for c in range(count):
        load_picked(c).start()
    for z in range(1, slots - 1):
        load(z, z).start()
    sums[...] = jnp.zeros_like(sums)
    for c in range(count):
        load_picked(c).wait()

    def step(z, _):
        slot = lax.rem(z, slots)

        @pl.when(z + slots - 1 < depth)
        def _():
            load(z + slots - 1, lax.rem(z + slots - 1, slots)).start()

        for c in range(count):
            at = (columns + c) * PITCH
            rows[at : at + height] = picked_slab[c, z].astype(F32)
        load(z, slot).wait()
        for c in range(columns):
            rows[c * PITCH : c * PITCH + height] = image_slab[slot, c].astype(F32)
        both = jnp.concatenate(
            [rows[pl.ds(y, total, stride=PITCH), :].astype(BF16) for y in range(height)], 1
        )
        sums[...] += lax.dot_general(both, both[:columns], NT, preferred_element_type=F32)
        return 0

    lax.fori_loop(0, depth, step, 0)


def coefficient(material):
    squared = jnp.where(
        material == 0, 0.3, jnp.where(material == 1, 0.9, jnp.where(material == 2, 1.6, 2.5))
    ).astype(F32)
    return 6.0 - squared


def beside_in_row(row, first, last):
    width = row.shape[1]
    up = jnp.where(first, 0.0, pltpu.roll(row, 1, 1))
    down = jnp.where(last, 0.0, pltpu.roll(row, width - 1, 1))
    return up + down


def normal_kernel(
    edges, sums, turned, material, z_low, z_high, y_low, y_high, packed, gram
):
    depth, height, columns, width = turned.shape
    count = sums.shape[0] - columns
    gram[...] = jnp.zeros_like(gram)
    lane = lax.broadcasted_iota(jnp.int32, (columns, width), 1)
    first, last = lane == 0, lane == width - 1
    inside = [edges[i].astype(F32) for i in range(4)]
    gap = jnp.zeros((16 - columns % 16, height * width), BF16)

    def plane(z, below, here, above, keep_below=None, keep_above=None):
        scale = coefficient(material[z])
        middle = [y_low[z].astype(F32) * inside[2], here[0].astype(F32)]
        highs, lows = [], []
        for y in range(height):
            if y == height - 1:
                middle.append(y_high[z].astype(F32) * inside[3])
            else:
                middle.append(here[y + 1].astype(F32))
            row = middle[y + 1]
            under, over = below[y].astype(F32), above[y].astype(F32)
            if keep_below is not None:
                under = under * keep_below
            if keep_above is not None:
                over = over * keep_above
            beside = under + over + (middle[y] + middle[y + 2])
            beside = beside + beside_in_row(row, first, last)
            image = scale[y : y + 1, :] * row - beside
            rounded = image.astype(BF16)
            highs.append(rounded)
            lows.append((image - rounded.astype(F32)).astype(BF16))
        rounded = jnp.concatenate(highs, 1)
        both = jnp.concatenate([rounded, gap, jnp.concatenate(lows, 1)], 0)
        part = lax.dot_general(both, rounded, NT, preferred_element_type=F32)
        gram[:columns] += part[:columns]
        gram[columns:] += part[both.shape[0] - columns :]

    def step(z, _):
        plane(z, turned.at[z - 1], turned.at[z], turned.at[z + 1])
        return 0

    lax.fori_loop(1, depth - 1, step, 0)
    plane(0, z_low, turned.at[0], turned.at[1], keep_below=inside[0])
    end = depth - 1
    plane(end, turned.at[end - 1], turned.at[end], z_high, keep_above=inside[1])
    side = jnp.zeros((columns, 128 - columns), F32)
    foot = jnp.zeros((128 - columns, 128), F32)
    cross = jnp.concatenate([gram[columns:], side], 1)
    cross_t = jnp.concatenate([cross, foot], 0).T[:columns]
    normal = jnp.concatenate([gram[:columns], side], 1) + cross + cross_t
    col = lax.broadcasted_iota(jnp.int32, (columns, 128), 1)
    line = lax.broadcasted_iota(jnp.int32, (columns, 128), 0)
    diagonal = jnp.sum(jnp.where(line == col, normal, 0.0), axis=1, keepdims=True)
    grams = sums[:columns]
    picked_t = jnp.concatenate(
        [jnp.concatenate([sums[columns:], jnp.zeros((count, 128 - columns), F32)], 1),
         jnp.zeros((128 - count, 128), F32)], 0
    ).T[:columns]
    placed = pltpu.roll(picked_t, columns, 1)
    grams = jnp.concatenate([grams, side], 1)
    out = jnp.where(line >= col, grams, normal)
    out = jnp.where(col >= columns, placed, out)
    packed[...] = jnp.where(col == columns + count, diagonal, out)


def spread(row, lane):
    return jnp.broadcast_to(row[:, lane : lane + 1], row.shape)


def eliminate(blocks, panel, followers):
    base = 8 * panel
    wide = blocks[panel].shape
    rows = [jnp.broadcast_to(blocks[panel][i : i + 1, :], wide) for i in range(8)]
    heads = [[spread(rows[i], base + j) for j in range(8)] for i in range(8)]
    forward, pivots = [], []
    for k in range(8):
        forward.append(rows[k])
        pivots.append(heads[k][k])
        inverse = 1.0 / heads[k][k]
        rows[k] = rows[k] * inverse
        for j in range(k + 1, 8):
            heads[k][j] = heads[k][j] * inverse
        for i in range(8):
            if i == k:
                continue
            factor = heads[i][k]
            rows[i] = rows[i] - factor * rows[k]
            for j in range(k + 1, 8):
                heads[i][j] = heads[i][j] - factor * heads[k][j]
    for i in followers:
        block = blocks[i]
        for j in range(8):
            block = block - spread(blocks[i], base + j) * rows[j]
        blocks[i] = block
    return rows, forward, pivots


def stacked(rows):
    line = lax.broadcasted_iota(jnp.int32, rows[0].shape, 0)
    out = rows[0]
    for i in range(1, 8):
        out = jnp.where(line == i, rows[i], out)
    return out


def combination(packed, columns, count):
    exact = lax.Precision.HIGHEST
    shape = (128, 128)
    col = lax.broadcasted_iota(jnp.int32, shape, 1)
    line = lax.broadcasted_iota(jnp.int32, shape, 0)
    full = jnp.concatenate([packed, jnp.zeros((128 - columns, 128), F32)], 0)
    flipped = full.T
    grams = jnp.where(line >= col, full, flipped)
    grams = jnp.where(col >= columns, full, grams)
    diagonal = jnp.broadcast_to(full[:, columns + count : columns + count + 1], shape)
    normal = jnp.where(line < col, full, flipped)
    normal = jnp.where(line == col, diagonal, normal)
    normal = jnp.where((col < columns) & (line < columns), normal, 0.0)
    blocks = [grams[8 * i : 8 * i + 8] for i in range(columns // 8)]
    for panel in range(len(blocks)):
        rest = [i for i in range(len(blocks)) if i != panel]
        rows, _, _ = eliminate(blocks, panel, rest)
        blocks[panel] = stacked(rows)
    solved = jnp.concatenate(blocks + [jnp.zeros((128 - columns, 128), F32)], 0)
    solved = pltpu.roll(solved, 128 - columns, 1)
    chosen = jnp.where(col < count, solved, 0.0).astype(BF16).astype(F32)
    chosen_t = chosen.T
    product = jnp.dot(normal, chosen, precision=exact, preferred_element_type=F32)
    normal = jnp.dot(chosen_t, product, precision=exact, preferred_element_type=F32)
    normal = normal[:count] * (1.0 / CELLS)
    joined = jnp.where(col[:count] < count, normal, pltpu.roll(chosen_t[:count], count, 1))
    blocks = [joined[8 * i : 8 * i + 8] for i in range(count // 8)]
    for panel in range(len(blocks)):
        rest = range(panel + 1, len(blocks))
        _, forward, pivots = eliminate(blocks, panel, rest)
        blocks[panel] = stacked([r * lax.rsqrt(d) for r, d in zip(forward, pivots)])
    return pltpu.roll(jnp.concatenate(blocks, 0), 128 - count, 1)[:, :columns]


def update_kernel(
    edges, packed, turned, material, z_low, z_high, y_low, y_high, recycle, images,
    planes, first_out, second_out, store_sems,
):
    depth, height, columns, width = turned.shape
    count = recycle.shape[0]
    weights = combination(packed[...], columns, count)
    rounded = weights.astype(BF16)
    both = jnp.concatenate([rounded, (weights - rounded.astype(F32)).astype(BF16)], 0)

    def combine(row):
        part = jnp.dot(both, row, preferred_element_type=F32)
        return part[:count] + part[count:]

    low = combine(jnp.concatenate([y_low[z] for z in range(depth)], 1))
    high = combine(jnp.concatenate([y_high[z] for z in range(depth)], 1))
    for z in range(depth):
        planes[z + 1, 0] = low[:, z * width : (z + 1) * width] * edges[2].astype(F32)
        planes[z + 1, height + 1] = high[:, z * width : (z + 1) * width] * edges[3].astype(F32)

    def fill(z, source, keep=None):
        plane = combine(jnp.concatenate([source[y] for y in range(height)], 1))
        if keep is not None:
            plane = plane * keep.astype(F32)
        for y in range(height):
            planes[z, y + 1] = plane[:, y * width : (y + 1) * width]

    def stores(z, slot):
        return (
            pltpu.make_async_copy(first_out.at[slot, :, :height], recycle.at[:, z], store_sems.at[slot, 0]),
            pltpu.make_async_copy(second_out.at[slot, :, :height], images.at[:, z], store_sems.at[slot, 1]),
        )

    fill(0, z_low, edges[0])
    fill(1, turned.at[0])
    lane = lax.broadcasted_iota(jnp.int32, (count, width), 1)
    first, last = lane == 0, lane == width - 1

    def step(z, _):
        slot = lax.rem(z, SLOTS)

        @pl.when(z + 1 < depth)
        def _():
            fill(z + 2, turned.at[z + 1])

        @pl.when(z + 1 == depth)
        def _():
            fill(z + 2, z_high, edges[1])

        @pl.when(z >= SLOTS)
        def _():
            for copy in stores(z - SLOTS, slot):
                copy.wait()

        scale = coefficient(material[z])
        one = first_out.at[slot].reshape(count * STEP, width)
        two = second_out.at[slot].reshape(count * STEP, width)
        for y in range(height):
            row = planes[z + 1, y + 1]
            beside = planes[z, y + 1] + planes[z + 2, y + 1]
            beside = beside + (planes[z + 1, y] + planes[z + 1, y + 2])
            beside = beside + beside_in_row(row, first, last)
            one[pl.ds(y, count, stride=STEP), :] = row
            two[pl.ds(y, count, stride=STEP), :] = scale[y : y + 1, :] * row - beside
        for copy in stores(z, slot):
            copy.start()
        return 0

    lax.fori_loop(0, depth, step, 0)
    for z in range(depth - SLOTS, depth):
        for copy in stores(z, z % SLOTS):
            copy.wait()


def device_sum(value):
    def shifted(axis, perm):
        return lax.ppermute(value, axis, perm)

    slabs = range(32)
    value = value + shifted("slab", [(i, i ^ 1) for i in slabs])
    for stride in (8, 2, 0):
        if stride:
            def move(i, d):
                place = (i // stride) % 4
                return i + ((place + d) % 4 - place) * stride
            axis, perms = "slab", [[(i, move(i, d)) for i in slabs] for d in (1, 2, 3)]
        else:
            axis = "pencil"
            perms = [[(i, (i + d) % 4) for i in range(4)] for d in (1, 2, 3)]
        left, opposite, right = [shifted(axis, perm) for perm in perms]
        value = (value + opposite) + (left + right)
    return value


def whole(memory=pltpu.VMEM):
    return pl.BlockSpec(memory_space=memory)


def local(basis, image, material, picked):
    columns, depth, height, width = basis.shape
    count = picked.shape[0]
    slabs, pencils = lax.axis_size("slab"), lax.axis_size("pencil")

    def neighbours(low_face, high_face, axis, size):
        up = [(i, (i + 1) % size) for i in range(size)]
        down = [(j, i) for i, j in up]
        return lax.ppermute(high_face, axis, up), lax.ppermute(low_face, axis, down)

    face = jax.ShapeDtypeStruct((height, columns, width), BF16)
    edge = jax.ShapeDtypeStruct((depth, columns, width), BF16)
    turned, z_first, z_last, y_first, y_last = pl.pallas_call(
        turn_kernel,
        in_specs=[whole(pltpu.HBM)],
        out_specs=[whole(pltpu.HBM)] + [whole()] * 4,
        out_shape=[jax.ShapeDtypeStruct((depth, height, columns, width), BF16), face, face, edge, edge],
        scratch_shapes=[
            pltpu.VMEM((3, columns, height, width), BF16),
            pltpu.VMEM((3, height, columns, width), BF16),
            pltpu.SemaphoreType.DMA((3,)),
            pltpu.SemaphoreType.DMA((3,)),
        ],
        compiler_params=pltpu.CompilerParams(vmem_limit_bytes=57 * MIB),
        name="turn",
    )(basis)
    z_low, z_high = neighbours(z_first, z_last, "slab", slabs)
    y_low, y_high = neighbours(y_first, y_last, "pencil", pencils)
    sums = pl.pallas_call(
        gram_kernel,
        in_specs=[whole(pltpu.SMEM), whole(pltpu.HBM), whole(pltpu.HBM)],
        out_specs=whole(),
        out_shape=jax.ShapeDtypeStruct((columns + count, columns), F32),
        scratch_shapes=[
            pltpu.VMEM((3, columns, height, width), BF16),
            pltpu.VMEM((count, depth, height, width), BF16),
            pltpu.VMEM(((columns + count) * PITCH, width), F32),
            pltpu.SemaphoreType.DMA((3,)),
            pltpu.SemaphoreType.DMA((count,)),
        ],
        compiler_params=pltpu.CompilerParams(vmem_limit_bytes=49 * MIB),
        cost_estimate=pl.CostEstimate(flops=2 * 10**9, bytes_accessed=17 * 10**6, transcendentals=0),
        name="gram",
    )(picked, image, basis)
    faces = (z_low, z_high, y_low, y_high)
    slab, pencil = lax.axis_index("slab"), lax.axis_index("pencil")
    inner = (slab > 0, slab < slabs - 1, pencil > 0, pencil < pencils - 1)
    edges = jnp.stack(inner).astype(jnp.int32)
    packed = pl.pallas_call(
        normal_kernel,
        in_specs=[whole(pltpu.SMEM)] + [whole()] * 7,
        out_specs=whole(),
        out_shape=jax.ShapeDtypeStruct((columns, 128), F32),
        scratch_shapes=[pltpu.VMEM((2 * columns, columns), F32)],
        compiler_params=pltpu.CompilerParams(vmem_limit_bytes=16 * MIB),
        name="normal",
    )(edges, sums, turned, material, *faces)
    packed = device_sum(packed)
    grid_shape = (count, depth, height, width)
    return pl.pallas_call(
        update_kernel,
        in_specs=[whole(pltpu.SMEM)] + [whole()] * 7,
        out_specs=[whole(pltpu.HBM), whole(pltpu.HBM)],
        out_shape=[jax.ShapeDtypeStruct(grid_shape, F32)] * 2,
        scratch_shapes=[
            pltpu.VMEM((depth + 2, height + 2, count, width), F32),
            pltpu.VMEM((SLOTS, count, STEP, width), F32),
            pltpu.VMEM((SLOTS, count, STEP, width), F32),
            pltpu.SemaphoreType.DMA((SLOTS, 2)),
        ],
        compiler_params=pltpu.CompilerParams(vmem_limit_bytes=20 * MIB),
        name="update",
    )(edges, packed, turned, material, *faces)


def solution(mesh):
    field = P(None, "slab", "pencil", None)
    return jax.shard_map(
        local,
        mesh=mesh,
        in_specs=(field, field, P("slab", "pencil", None), P()),
        out_specs=(field, field),
        check_vma=False,
    )
```

```python
import jax
import jax.numpy as jnp
from jax import lax
from jax.experimental import pallas as pl
from jax.experimental.pallas import tpu as pltpu
from jax.sharding import PartitionSpec as P

F32 = jnp.float32
BF16 = jnp.bfloat16
CELLS = 4194304.0
PITCH = 44
STEP = 40
SLOTS = 2
NT = (((1,), (1,)), ((), ()))
TN = (((0,), (0,)), ((), ()))
MIB = 2**20


def face_kernel(basis, z_first, z_last, y_first, y_last, slab, sems):
    depth, height = basis.shape[1:3]
    slots = slab.shape[0]

    def load(z, slot):
        return pltpu.make_async_copy(basis.at[:, z], slab.at[slot], sems.at[slot])

    for z in range(slots - 1):
        load(z, z).start()

    def step(z, _):
        slot = lax.rem(z, slots)

        @pl.when(z + slots - 1 < depth)
        def _():
            load(z + slots - 1, lax.rem(z + slots - 1, slots)).start()

        load(z, slot).wait()
        y_first[z] = jnp.swapaxes(slab[slot, :, :16, :], 0, 1)[0]
        y_last[z] = jnp.swapaxes(slab[slot, :, height - 16 :, :], 0, 1)[15]

        def whole_plane(face):
            for y in range(0, height, 16):
                face[y : y + 16] = jnp.swapaxes(slab[slot, :, y : y + 16, :], 0, 1)

        pl.when(z == 0)(lambda: whole_plane(z_first))
        pl.when(z == depth - 1)(lambda: whole_plane(z_last))
        return 0

    lax.fori_loop(0, depth, step, 0)


def gram_kernel(
    picked, image, basis, sums, turned, image_slab, basis_slab, rows, image_sems, basis_sems
):
    columns, depth, height, width = image.shape
    count = picked.shape[0]
    total = columns + count
    slots = image_slab.shape[0]

    def loads(z, slot):
        return (
            pltpu.make_async_copy(image.at[:, z], image_slab.at[slot], image_sems.at[slot]),
            pltpu.make_async_copy(basis.at[:, z], basis_slab.at[slot], basis_sems.at[slot]),
        )

    for z in range(slots - 1):
        for copy in loads(z, z):
            copy.start()
    sums[...] = jnp.zeros_like(sums)

    def step(z, _):
        slot = lax.rem(z, slots)

        @pl.when(z + slots - 1 < depth)
        def _():
            for copy in loads(z + slots - 1, lax.rem(z + slots - 1, slots)):
                copy.start()

        for copy in loads(z, slot):
            copy.wait()
        for c in range(columns):
            rows[c * PITCH : c * PITCH + height] = image_slab[slot, c].astype(F32)
        for c in range(count):
            at = (columns + c) * PITCH
            rows[at : at + height] = basis_slab[slot, picked[c]].astype(F32)
        for y in range(0, height, 16):
            turned[z, y : y + 16] = jnp.swapaxes(basis_slab[slot, :, y : y + 16, :], 0, 1)
        both = jnp.concatenate(
            [rows[pl.ds(y, total, stride=PITCH), :].astype(BF16) for y in range(height)], 1
        )
        sums[...] += lax.dot_general(both, both[:columns], NT, preferred_element_type=F32)
        return 0

    lax.fori_loop(0, depth, step, 0)


def coefficient(material):
    squared = jnp.where(
        material == 0, 0.3, jnp.where(material == 1, 0.9, jnp.where(material == 2, 1.6, 2.5))
    ).astype(F32)
    return 6.0 - squared


def beside_in_row(row, first, last):
    width = row.shape[1]
    up = jnp.where(first, 0.0, pltpu.roll(row, 1, 1))
    down = jnp.where(last, 0.0, pltpu.roll(row, width - 1, 1))
    return up + down


def normal_kernel(
    edges, sums, turned, material, z_low, z_high, y_low, y_high, packed, gram
):
    depth, height, columns, width = turned.shape
    count = sums.shape[0] - columns
    gram[...] = jnp.zeros_like(gram)
    lane = lax.broadcasted_iota(jnp.int32, (columns, width), 1)
    first, last = lane == 0, lane == width - 1
    inside = [edges[i].astype(F32) for i in range(4)]
    gap = jnp.zeros((16 - columns % 16, height * width), BF16)

    def plane(z, below, here, above, keep_below=None, keep_above=None):
        scale = coefficient(material[z])
        middle = [y_low[z].astype(F32) * inside[2], here[0].astype(F32)]
        highs, lows = [], []
        for y in range(height):
            if y == height - 1:
                middle.append(y_high[z].astype(F32) * inside[3])
            else:
                middle.append(here[y + 1].astype(F32))
            row = middle[y + 1]
            under, over = below[y].astype(F32), above[y].astype(F32)
            if keep_below is not None:
                under = under * keep_below
            if keep_above is not None:
                over = over * keep_above
            beside = under + over + (middle[y] + middle[y + 2])
            beside = beside + beside_in_row(row, first, last)
            image = scale[y : y + 1, :] * row - beside
            rounded = image.astype(BF16)
            highs.append(rounded)
            lows.append((image - rounded.astype(F32)).astype(BF16))
        rounded = jnp.concatenate(highs, 1)
        both = jnp.concatenate([rounded, gap, jnp.concatenate(lows, 1)], 0)
        part = lax.dot_general(both, rounded, NT, preferred_element_type=F32)
        gram[:columns] += part[:columns]
        gram[columns:] += part[both.shape[0] - columns :]

    def step(z, _):
        plane(z, turned.at[z - 1], turned.at[z], turned.at[z + 1])
        return 0

    lax.fori_loop(1, depth - 1, step, 0)
    plane(0, z_low, turned.at[0], turned.at[1], keep_below=inside[0])
    end = depth - 1
    plane(end, turned.at[end - 1], turned.at[end], z_high, keep_above=inside[1])
    side = jnp.zeros((columns, 128 - columns), F32)
    foot = jnp.zeros((128 - columns, 128), F32)
    cross = jnp.concatenate([gram[columns:], side], 1)
    cross_t = jnp.concatenate([cross, foot], 0).T[:columns]
    normal = jnp.concatenate([gram[:columns], side], 1) + cross + cross_t
    col = lax.broadcasted_iota(jnp.int32, (columns, 128), 1)
    line = lax.broadcasted_iota(jnp.int32, (columns, 128), 0)
    diagonal = jnp.sum(jnp.where(line == col, normal, 0.0), axis=1, keepdims=True)
    grams = sums[:columns]
    picked_t = jnp.concatenate(
        [jnp.concatenate([sums[columns:], jnp.zeros((count, 128 - columns), F32)], 1),
         jnp.zeros((128 - count, 128), F32)], 0
    ).T[:columns]
    placed = pltpu.roll(picked_t, columns, 1)
    grams = jnp.concatenate([grams, side], 1)
    out = jnp.where(line >= col, grams, normal)
    out = jnp.where(col >= columns, placed, out)
    packed[...] = jnp.where(col == columns + count, diagonal, out)


def spread(row, lane):
    return jnp.broadcast_to(row[:, lane : lane + 1], row.shape)


def eliminate(blocks, panel, followers):
    base = 8 * panel
    wide = blocks[panel].shape
    rows = [jnp.broadcast_to(blocks[panel][i : i + 1, :], wide) for i in range(8)]
    heads = [[spread(rows[i], base + j) for j in range(8)] for i in range(8)]
    forward, pivots = [], []
    for k in range(8):
        forward.append(rows[k])
        pivots.append(heads[k][k])
        inverse = 1.0 / heads[k][k]
        rows[k] = rows[k] * inverse
        for j in range(k + 1, 8):
            heads[k][j] = heads[k][j] * inverse
        for i in range(8):
            if i == k:
                continue
            factor = heads[i][k]
            rows[i] = rows[i] - factor * rows[k]
            for j in range(k + 1, 8):
                heads[i][j] = heads[i][j] - factor * heads[k][j]
    for i in followers:
        block = blocks[i]
        for j in range(8):
            block = block - spread(blocks[i], base + j) * rows[j]
        blocks[i] = block
    return rows, forward, pivots


def stacked(rows):
    line = lax.broadcasted_iota(jnp.int32, rows[0].shape, 0)
    out = rows[0]
    for i in range(1, 8):
        out = jnp.where(line == i, rows[i], out)
    return out


def combination(packed, columns, count):
    exact = lax.Precision.HIGHEST
    shape = (128, 128)
    col = lax.broadcasted_iota(jnp.int32, shape, 1)
    line = lax.broadcasted_iota(jnp.int32, shape, 0)
    full = jnp.concatenate([packed, jnp.zeros((128 - columns, 128), F32)], 0)
    flipped = full.T
    grams = jnp.where(line >= col, full, flipped)
    grams = jnp.where(col >= columns, full, grams)
    diagonal = jnp.broadcast_to(full[:, columns + count : columns + count + 1], shape)
    normal = jnp.where(line < col, full, flipped)
    normal = jnp.where(line == col, diagonal, normal)
    normal = jnp.where((col < columns) & (line < columns), normal, 0.0)
    blocks = [grams[8 * i : 8 * i + 8] for i in range(columns // 8)]
    for panel in range(len(blocks)):
        rest = [i for i in range(len(blocks)) if i != panel]
        rows, _, _ = eliminate(blocks, panel, rest)
        blocks[panel] = stacked(rows)
    solved = jnp.concatenate(blocks + [jnp.zeros((128 - columns, 128), F32)], 0)
    solved = pltpu.roll(solved, 128 - columns, 1)
    chosen = jnp.where(col < count, solved, 0.0).astype(BF16).astype(F32)
    chosen_t = chosen.T
    product = jnp.dot(normal, chosen, precision=exact, preferred_element_type=F32)
    normal = jnp.dot(chosen_t, product, precision=exact, preferred_element_type=F32)
    normal = normal[:count] * (1.0 / CELLS)
    joined = jnp.where(col[:count] < count, normal, pltpu.roll(chosen_t[:count], count, 1))
    blocks = [joined[8 * i : 8 * i + 8] for i in range(count // 8)]
    for panel in range(len(blocks)):
        rest = range(panel + 1, len(blocks))
        _, forward, pivots = eliminate(blocks, panel, rest)
        blocks[panel] = stacked([r * lax.rsqrt(d) for r, d in zip(forward, pivots)])
    return pltpu.roll(jnp.concatenate(blocks, 0), 128 - count, 1)[:, :columns]


def update_kernel(
    edges, packed, turned, material, z_low, z_high, y_low, y_high, recycle, images,
    planes, first_out, second_out, store_sems,
):
    depth, height, columns, width = turned.shape
    count = recycle.shape[0]
    weights = combination(packed[...], columns, count)
    rounded = weights.astype(BF16)
    both = jnp.concatenate([rounded, (weights - rounded.astype(F32)).astype(BF16)], 0)

    def combine(row):
        part = jnp.dot(both, row, preferred_element_type=F32)
        return part[:count] + part[count:]

    low = combine(jnp.concatenate([y_low[z] for z in range(depth)], 1))
    high = combine(jnp.concatenate([y_high[z] for z in range(depth)], 1))
    for z in range(depth):
        planes[z + 1, 0] = low[:, z * width : (z + 1) * width] * edges[2].astype(F32)
        planes[z + 1, height + 1] = high[:, z * width : (z + 1) * width] * edges[3].astype(F32)

    def fill(z, source, keep=None):
        plane = combine(jnp.concatenate([source[y] for y in range(height)], 1))
        if keep is not None:
            plane = plane * keep.astype(F32)
        for y in range(height):
            planes[z, y + 1] = plane[:, y * width : (y + 1) * width]

    def stores(z, slot):
        return (
            pltpu.make_async_copy(first_out.at[slot, :, :height], recycle.at[:, z], store_sems.at[slot, 0]),
            pltpu.make_async_copy(second_out.at[slot, :, :height], images.at[:, z], store_sems.at[slot, 1]),
        )

    fill(0, z_low, edges[0])
    fill(1, turned.at[0])
    lane = lax.broadcasted_iota(jnp.int32, (count, width), 1)
    first, last = lane == 0, lane == width - 1

    def step(z, _):
        slot = lax.rem(z, SLOTS)

        @pl.when(z + 1 < depth)
        def _():
            fill(z + 2, turned.at[z + 1])

        @pl.when(z + 1 == depth)
        def _():
            fill(z + 2, z_high, edges[1])

        @pl.when(z >= SLOTS)
        def _():
            for copy in stores(z - SLOTS, slot):
                copy.wait()

        scale = coefficient(material[z])
        one = first_out.at[slot].reshape(count * STEP, width)
        two = second_out.at[slot].reshape(count * STEP, width)
        for y in range(height):
            row = planes[z + 1, y + 1]
            beside = planes[z, y + 1] + planes[z + 2, y + 1]
            beside = beside + (planes[z + 1, y] + planes[z + 1, y + 2])
            beside = beside + beside_in_row(row, first, last)
            one[pl.ds(y, count, stride=STEP), :] = row
            two[pl.ds(y, count, stride=STEP), :] = scale[y : y + 1, :] * row - beside
        for copy in stores(z, slot):
            copy.start()
        return 0

    lax.fori_loop(0, depth, step, 0)
    for z in range(depth - SLOTS, depth):
        for copy in stores(z, z % SLOTS):
            copy.wait()


def device_sum(value):
    def shifted(axis, perm):
        return lax.ppermute(value, axis, perm)

    slabs = range(32)
    value = value + shifted("slab", [(i, i ^ 1) for i in slabs])
    for stride in (8, 2, 0):
        if stride:
            def move(i, d):
                place = (i // stride) % 4
                return i + ((place + d) % 4 - place) * stride
            axis, perms = "slab", [[(i, move(i, d)) for i in slabs] for d in (1, 2, 3)]
        else:
            axis = "pencil"
            perms = [[(i, (i + d) % 4) for i in range(4)] for d in (1, 2, 3)]
        left, opposite, right = [shifted(axis, perm) for perm in perms]
        value = (value + opposite) + (left + right)
    return value


def whole(memory=pltpu.VMEM):
    return pl.BlockSpec(memory_space=memory)


def local(basis, image, material, picked):
    columns, depth, height, width = basis.shape
    count = picked.shape[0]
    slabs, pencils = lax.axis_size("slab"), lax.axis_size("pencil")

    def neighbours(low_face, high_face, axis, size):
        up = [(i, (i + 1) % size) for i in range(size)]
        down = [(j, i) for i, j in up]
        return lax.ppermute(high_face, axis, up), lax.ppermute(low_face, axis, down)

    face = jax.ShapeDtypeStruct((height, columns, width), BF16)
    edge = jax.ShapeDtypeStruct((depth, columns, width), BF16)
    z_first, z_last, y_first, y_last = pl.pallas_call(
        face_kernel,
        in_specs=[whole(pltpu.HBM)],
        out_specs=[whole()] * 4,
        out_shape=[face, face, edge, edge],
        scratch_shapes=[
            pltpu.VMEM((4, columns, height, width), BF16),
            pltpu.SemaphoreType.DMA((4,)),
        ],
        compiler_params=pltpu.CompilerParams(vmem_limit_bytes=52 * MIB),
        name="faces",
    )(basis)
    z_low, z_high = neighbours(z_first, z_last, "slab", slabs)
    y_low, y_high = neighbours(y_first, y_last, "pencil", pencils)
    sums, turned = pl.pallas_call(
        gram_kernel,
        in_specs=[whole(pltpu.SMEM), whole(pltpu.HBM), whole(pltpu.HBM)],
        out_specs=[whole()] * 2,
        out_shape=[
            jax.ShapeDtypeStruct((columns + count, columns), F32),
            jax.ShapeDtypeStruct((depth, height, columns, width), BF16),
        ],
        scratch_shapes=[
            pltpu.VMEM((4, columns, height, width), BF16),
            pltpu.VMEM((4, columns, height, width), BF16),
            pltpu.VMEM(((columns + count) * PITCH, width), F32),
            pltpu.SemaphoreType.DMA((4,)),
            pltpu.SemaphoreType.DMA((4,)),
        ],
        compiler_params=pltpu.CompilerParams(vmem_limit_bytes=46 * MIB),
        cost_estimate=pl.CostEstimate(flops=2 * 10**9, bytes_accessed=17 * 10**6, transcendentals=0),
        name="gram",
    )(picked, image, basis)
    faces = (z_low, z_high, y_low, y_high)
    slab, pencil = lax.axis_index("slab"), lax.axis_index("pencil")
    inner = (slab > 0, slab < slabs - 1, pencil > 0, pencil < pencils - 1)
    edges = jnp.stack(inner).astype(jnp.int32)
    packed = pl.pallas_call(
        normal_kernel,
        in_specs=[whole(pltpu.SMEM)] + [whole()] * 7,
        out_specs=whole(),
        out_shape=jax.ShapeDtypeStruct((columns, 128), F32),
        scratch_shapes=[pltpu.VMEM((2 * columns, columns), F32)],
        compiler_params=pltpu.CompilerParams(vmem_limit_bytes=16 * MIB),
        name="normal",
    )(edges, sums, turned, material, *faces)
    packed = device_sum(packed)
    grid_shape = (count, depth, height, width)
    return pl.pallas_call(
        update_kernel,
        in_specs=[whole(pltpu.SMEM)] + [whole()] * 7,
        out_specs=[whole(pltpu.HBM), whole(pltpu.HBM)],
        out_shape=[jax.ShapeDtypeStruct(grid_shape, F32)] * 2,
        scratch_shapes=[
            pltpu.VMEM((depth + 2, height + 2, count, width), F32),
            pltpu.VMEM((SLOTS, count, STEP, width), F32),
            pltpu.VMEM((SLOTS, count, STEP, width), F32),
            pltpu.SemaphoreType.DMA((SLOTS, 2)),
        ],
        compiler_params=pltpu.CompilerParams(vmem_limit_bytes=20 * MIB),
        name="update",
    )(edges, packed, turned, material, *faces)


def solution(mesh):
    field = P(None, "slab", "pencil", None)
    return jax.shard_map(
        local,
        mesh=mesh,
        in_specs=(field, field, P("slab", "pencil", None), P()),
        out_specs=(field, field),
        check_vma=False,
    )
```

```python
import jax
import jax.numpy as jnp
from jax import lax
from jax.experimental import pallas as pl
from jax.experimental.pallas import tpu as pltpu
from jax.sharding import PartitionSpec as P

F32 = jnp.float32
BF16 = jnp.bfloat16
CELLS = 4194304.0
PITCH = 44
STEP = 40
SLOTS = 2
NT = (((1,), (1,)), ((), ()))
TN = (((0,), (0,)), ((), ()))
MIB = 2**20


def face_kernel(basis, z_first, z_last, y_first, y_last, slab, sems):
    depth, height = basis.shape[1:3]
    slots = slab.shape[0]

    def load(z, slot):
        return pltpu.make_async_copy(basis.at[:, z], slab.at[slot], sems.at[slot])

    for z in range(slots - 1):
        load(z, z).start()

    def step(z, _):
        slot = lax.rem(z, slots)

        @pl.when(z + slots - 1 < depth)
        def _():
            load(z + slots - 1, lax.rem(z + slots - 1, slots)).start()

        load(z, slot).wait()
        y_first[z] = jnp.swapaxes(slab[slot, :, :16, :], 0, 1)[0]
        y_last[z] = jnp.swapaxes(slab[slot, :, height - 16 :, :], 0, 1)[15]

        def whole_plane(face):
            for y in range(0, height, 16):
                face[y : y + 16] = jnp.swapaxes(slab[slot, :, y : y + 16, :], 0, 1)

        pl.when(z == 0)(lambda: whole_plane(z_first))
        pl.when(z == depth - 1)(lambda: whole_plane(z_last))
        return 0

    lax.fori_loop(0, depth, step, 0)


def gram_kernel(
    picked, image, basis, sums, turned, image_slab, basis_slab, rows, image_sems, basis_sems
):
    columns, depth, height, width = image.shape
    count = picked.shape[0]
    total = columns + count
    slots = image_slab.shape[0]

    def loads(z, slot):
        return (
            pltpu.make_async_copy(image.at[:, z], image_slab.at[slot], image_sems.at[slot]),
            pltpu.make_async_copy(basis.at[:, z], basis_slab.at[slot], basis_sems.at[slot]),
        )

    for z in range(slots - 1):
        for copy in loads(z, z):
            copy.start()
    sums[...] = jnp.zeros_like(sums)

    def step(z, _):
        slot = lax.rem(z, slots)

        @pl.when(z + slots - 1 < depth)
        def _():
            for copy in loads(z + slots - 1, lax.rem(z + slots - 1, slots)):
                copy.start()

        for copy in loads(z, slot):
            copy.wait()
        for c in range(columns):
            rows[c * PITCH : c * PITCH + height] = image_slab[slot, c].astype(F32)
        for c in range(count):
            at = (columns + c) * PITCH
            rows[at : at + height] = basis_slab[slot, picked[c]].astype(F32)
        for y in range(0, height, 16):
            turned[z, y : y + 16] = jnp.swapaxes(basis_slab[slot, :, y : y + 16, :], 0, 1)
        both = jnp.concatenate(
            [rows[pl.ds(y, total, stride=PITCH), :].astype(BF16) for y in range(height)], 1
        )
        sums[...] += lax.dot_general(both, both[:columns], NT, preferred_element_type=F32)
        return 0

    lax.fori_loop(0, depth, step, 0)


def coefficient(material):
    squared = jnp.where(
        material == 0, 0.3, jnp.where(material == 1, 0.9, jnp.where(material == 2, 1.6, 2.5))
    ).astype(F32)
    return 6.0 - squared


def beside_in_row(row, first, last):
    width = row.shape[1]
    up = jnp.where(first, 0.0, pltpu.roll(row, 1, 1))
    down = jnp.where(last, 0.0, pltpu.roll(row, width - 1, 1))
    return up + down


def add_plane(gram, scale, below, here, above, before, after, keeps):
    height, columns, width = here.shape
    lane = lax.broadcasted_iota(jnp.int32, (columns, width), 1)
    first, last = lane == 0, lane == width - 1
    middle = [before.astype(F32) * keeps[2], here[0].astype(F32)]
    highs, lows = [], []
    for y in range(height):
        if y == height - 1:
            middle.append(after.astype(F32) * keeps[3])
        else:
            middle.append(here[y + 1].astype(F32))
        row = middle[y + 1]
        under, over = below[y].astype(F32), above[y].astype(F32)
        if keeps[0] is not None:
            under = under * keeps[0]
        if keeps[1] is not None:
            over = over * keeps[1]
        beside = under + over + (middle[y] + middle[y + 2])
        beside = beside + beside_in_row(row, first, last)
        image = scale[y : y + 1, :] * row - beside
        rounded = image.astype(BF16)
        highs.append(rounded)
        lows.append((image - rounded.astype(F32)).astype(BF16))
    gap = jnp.zeros((16 - columns % 16, height * width), BF16)
    rounded = jnp.concatenate(highs, 1)
    both = jnp.concatenate([rounded, gap, jnp.concatenate(lows, 1)], 0)
    part = lax.dot_general(both, rounded, NT, preferred_element_type=F32)
    gram[:columns] += part[:columns]
    gram[columns:] += part[both.shape[0] - columns :]


def inner_kernel(edges, turned, material, y_low, y_high, gram):
    depth = turned.shape[0]
    gram[...] = jnp.zeros_like(gram)
    keeps = (None, None, edges[2].astype(F32), edges[3].astype(F32))

    def step(z, _):
        planes = (turned.at[z - 1], turned.at[z], turned.at[z + 1])
        add_plane(gram, coefficient(material[z]), *planes, y_low[z], y_high[z], keeps)
        return 0

    lax.fori_loop(1, depth - 1, step, 0)


def outer_kernel(
    edges, sums, part, turned, material, z_low, z_high, y_low, y_high, packed, gram
):
    depth, height, columns, width = turned.shape
    count = sums.shape[0] - columns
    gram[...] = part[...]
    inside = [edges[i].astype(F32) for i in range(4)]
    for z, planes, keeps in (
        (0, (z_low, turned.at[0], turned.at[1]), (inside[0], None)),
        (depth - 1, (turned.at[depth - 2], turned.at[depth - 1], z_high), (None, inside[1])),
    ):
        keeps = keeps + (inside[2], inside[3])
        add_plane(gram, coefficient(material[z]), *planes, y_low[z], y_high[z], keeps)
    side = jnp.zeros((columns, 128 - columns), F32)
    foot = jnp.zeros((128 - columns, 128), F32)
    cross = jnp.concatenate([gram[columns:], side], 1)
    cross_t = jnp.concatenate([cross, foot], 0).T[:columns]
    normal = jnp.concatenate([gram[:columns], side], 1) + cross + cross_t
    col = lax.broadcasted_iota(jnp.int32, (columns, 128), 1)
    line = lax.broadcasted_iota(jnp.int32, (columns, 128), 0)
    diagonal = jnp.sum(jnp.where(line == col, normal, 0.0), axis=1, keepdims=True)
    grams = sums[:columns]
    picked_t = jnp.concatenate(
        [jnp.concatenate([sums[columns:], jnp.zeros((count, 128 - columns), F32)], 1),
         jnp.zeros((128 - count, 128), F32)], 0
    ).T[:columns]
    placed = pltpu.roll(picked_t, columns, 1)
    grams = jnp.concatenate([grams, side], 1)
    out = jnp.where(line >= col, grams, normal)
    out = jnp.where(col >= columns, placed, out)
    packed[...] = jnp.where(col == columns + count, diagonal, out)


def spread(row, lane):
    return jnp.broadcast_to(row[:, lane : lane + 1], row.shape)


def eliminate(blocks, panel, followers):
    base = 8 * panel
    wide = blocks[panel].shape
    rows = [jnp.broadcast_to(blocks[panel][i : i + 1, :], wide) for i in range(8)]
    heads = [[spread(rows[i], base + j) for j in range(8)] for i in range(8)]
    forward, pivots = [], []
    for k in range(8):
        forward.append(rows[k])
        pivots.append(heads[k][k])
        inverse = 1.0 / heads[k][k]
        rows[k] = rows[k] * inverse
        for j in range(k + 1, 8):
            heads[k][j] = heads[k][j] * inverse
        for i in range(8):
            if i == k:
                continue
            factor = heads[i][k]
            rows[i] = rows[i] - factor * rows[k]
            for j in range(k + 1, 8):
                heads[i][j] = heads[i][j] - factor * heads[k][j]
    for i in followers:
        block = blocks[i]
        for j in range(8):
            block = block - spread(blocks[i], base + j) * rows[j]
        blocks[i] = block
    return rows, forward, pivots


def stacked(rows):
    line = lax.broadcasted_iota(jnp.int32, rows[0].shape, 0)
    out = rows[0]
    for i in range(1, 8):
        out = jnp.where(line == i, rows[i], out)
    return out


def combination(packed, columns, count):
    exact = lax.Precision.HIGHEST
    shape = (128, 128)
    col = lax.broadcasted_iota(jnp.int32, shape, 1)
    line = lax.broadcasted_iota(jnp.int32, shape, 0)
    full = jnp.concatenate([packed, jnp.zeros((128 - columns, 128), F32)], 0)
    flipped = full.T
    grams = jnp.where(line >= col, full, flipped)
    grams = jnp.where(col >= columns, full, grams)
    diagonal = jnp.broadcast_to(full[:, columns + count : columns + count + 1], shape)
    normal = jnp.where(line < col, full, flipped)
    normal = jnp.where(line == col, diagonal, normal)
    normal = jnp.where((col < columns) & (line < columns), normal, 0.0)
    blocks = [grams[8 * i : 8 * i + 8] for i in range(columns // 8)]
    for panel in range(len(blocks)):
        rest = [i for i in range(len(blocks)) if i != panel]
        rows, _, _ = eliminate(blocks, panel, rest)
        blocks[panel] = stacked(rows)
    solved = jnp.concatenate(blocks + [jnp.zeros((128 - columns, 128), F32)], 0)
    solved = pltpu.roll(solved, 128 - columns, 1)
    chosen = jnp.where(col < count, solved, 0.0).astype(BF16).astype(F32)
    chosen_t = chosen.T
    product = jnp.dot(normal, chosen, precision=exact, preferred_element_type=F32)
    normal = jnp.dot(chosen_t, product, precision=exact, preferred_element_type=F32)
    normal = normal[:count] * (1.0 / CELLS)
    joined = jnp.where(col[:count] < count, normal, pltpu.roll(chosen_t[:count], count, 1))
    blocks = [joined[8 * i : 8 * i + 8] for i in range(count // 8)]
    for panel in range(len(blocks)):
        rest = range(panel + 1, len(blocks))
        _, forward, pivots = eliminate(blocks, panel, rest)
        blocks[panel] = stacked([r * lax.rsqrt(d) for r, d in zip(forward, pivots)])
    return pltpu.roll(jnp.concatenate(blocks, 0), 128 - count, 1)[:, :columns]


def update_kernel(
    edges, packed, turned, material, z_low, z_high, y_low, y_high, recycle, images,
    planes, first_out, second_out, store_sems,
):
    depth, height, columns, width = turned.shape
    count = recycle.shape[0]
    weights = combination(packed[...], columns, count)
    rounded = weights.astype(BF16)
    both = jnp.concatenate([rounded, (weights - rounded.astype(F32)).astype(BF16)], 0)

    def combine(row):
        part = jnp.dot(both, row, preferred_element_type=F32)
        return part[:count] + part[count:]

    low = combine(jnp.concatenate([y_low[z] for z in range(depth)], 1))
    high = combine(jnp.concatenate([y_high[z] for z in range(depth)], 1))
    for z in range(depth):
        planes[z + 1, 0] = low[:, z * width : (z + 1) * width] * edges[2].astype(F32)
        planes[z + 1, height + 1] = high[:, z * width : (z + 1) * width] * edges[3].astype(F32)

    def fill(z, source, keep=None):
        plane = combine(jnp.concatenate([source[y] for y in range(height)], 1))
        if keep is not None:
            plane = plane * keep.astype(F32)
        for y in range(height):
            planes[z, y + 1] = plane[:, y * width : (y + 1) * width]

    def stores(z, slot):
        return (
            pltpu.make_async_copy(first_out.at[slot, :, :height], recycle.at[:, z], store_sems.at[slot, 0]),
            pltpu.make_async_copy(second_out.at[slot, :, :height], images.at[:, z], store_sems.at[slot, 1]),
        )

    fill(0, z_low, edges[0])
    fill(1, turned.at[0])
    lane = lax.broadcasted_iota(jnp.int32, (count, width), 1)
    first, last = lane == 0, lane == width - 1

    def step(z, _):
        slot = lax.rem(z, SLOTS)

        @pl.when(z + 1 < depth)
        def _():
            fill(z + 2, turned.at[z + 1])

        @pl.when(z + 1 == depth)
        def _():
            fill(z + 2, z_high, edges[1])

        @pl.when(z >= SLOTS)
        def _():
            for copy in stores(z - SLOTS, slot):
                copy.wait()

        scale = coefficient(material[z])
        one = first_out.at[slot].reshape(count * STEP, width)
        two = second_out.at[slot].reshape(count * STEP, width)
        for y in range(height):
            row = planes[z + 1, y + 1]
            beside = planes[z, y + 1] + planes[z + 2, y + 1]
            beside = beside + (planes[z + 1, y] + planes[z + 1, y + 2])
            beside = beside + beside_in_row(row, first, last)
            one[pl.ds(y, count, stride=STEP), :] = row
            two[pl.ds(y, count, stride=STEP), :] = scale[y : y + 1, :] * row - beside
        for copy in stores(z, slot):
            copy.start()
        return 0

    lax.fori_loop(0, depth, step, 0)
    for z in range(depth - SLOTS, depth):
        for copy in stores(z, z % SLOTS):
            copy.wait()


def device_sum(value):
    def exchanged(axis, size, distance):
        return lax.ppermute(value, axis, [(i, i ^ distance) for i in range(size)])

    value = value + exchanged("slab", 32, 1)
    for axis, size, stride in (("slab", 32, 8), ("slab", 32, 2), ("pencil", 4, 1)):
        near, opposite, far = [exchanged(axis, size, d * stride) for d in (1, 2, 3)]
        value = (value + opposite) + (near + far)
    return value


def whole(memory=pltpu.VMEM):
    return pl.BlockSpec(memory_space=memory)


def local(basis, image, material, picked):
    columns, depth, height, width = basis.shape
    count = picked.shape[0]
    slabs, pencils = lax.axis_size("slab"), lax.axis_size("pencil")

    def neighbours(low_face, high_face, axis, size):
        up = [(i, (i + 1) % size) for i in range(size)]
        down = [(j, i) for i, j in up]
        return lax.ppermute(high_face, axis, up), lax.ppermute(low_face, axis, down)

    face = jax.ShapeDtypeStruct((height, columns, width), BF16)
    edge = jax.ShapeDtypeStruct((depth, columns, width), BF16)
    z_first, z_last, y_first, y_last = pl.pallas_call(
        face_kernel,
        in_specs=[whole(pltpu.HBM)],
        out_specs=[whole()] * 4,
        out_shape=[face, face, edge, edge],
        scratch_shapes=[
            pltpu.VMEM((4, columns, height, width), BF16),
            pltpu.SemaphoreType.DMA((4,)),
        ],
        compiler_params=pltpu.CompilerParams(vmem_limit_bytes=52 * MIB),
        name="faces",
    )(basis)
    z_low, z_high = neighbours(z_first, z_last, "slab", slabs)
    y_low, y_high = neighbours(y_first, y_last, "pencil", pencils)
    sums, turned = pl.pallas_call(
        gram_kernel,
        in_specs=[whole(pltpu.SMEM), whole(pltpu.HBM), whole(pltpu.HBM)],
        out_specs=[whole()] * 2,
        out_shape=[
            jax.ShapeDtypeStruct((columns + count, columns), F32),
            jax.ShapeDtypeStruct((depth, height, columns, width), BF16),
        ],
        scratch_shapes=[
            pltpu.VMEM((4, columns, height, width), BF16),
            pltpu.VMEM((4, columns, height, width), BF16),
            pltpu.VMEM(((columns + count) * PITCH, width), F32),
            pltpu.SemaphoreType.DMA((4,)),
            pltpu.SemaphoreType.DMA((4,)),
        ],
        compiler_params=pltpu.CompilerParams(vmem_limit_bytes=46 * MIB),
        cost_estimate=pl.CostEstimate(flops=2 * 10**9, bytes_accessed=17 * 10**6, transcendentals=0),
        name="gram",
    )(picked, image, basis)
    faces = (z_low, z_high, y_low, y_high)
    slab, pencil = lax.axis_index("slab"), lax.axis_index("pencil")
    inner = (slab > 0, slab < slabs - 1, pencil > 0, pencil < pencils - 1)
    edges = jnp.stack(inner).astype(jnp.int32)
    grams = jax.ShapeDtypeStruct((2 * columns, columns), F32)
    part = pl.pallas_call(
        inner_kernel,
        in_specs=[whole(pltpu.SMEM)] + [whole()] * 4,
        out_specs=whole(),
        out_shape=grams,
        compiler_params=pltpu.CompilerParams(vmem_limit_bytes=16 * MIB),
        cost_estimate=pl.CostEstimate(flops=10**10, bytes_accessed=10**7, transcendentals=0),
        name="inner",
    )(edges, turned, material, y_low, y_high)
    packed = pl.pallas_call(
        outer_kernel,
        in_specs=[whole(pltpu.SMEM)] + [whole()] * 8,
        out_specs=whole(),
        out_shape=jax.ShapeDtypeStruct((columns, 128), F32),
        scratch_shapes=[pltpu.VMEM(grams.shape, F32)],
        compiler_params=pltpu.CompilerParams(vmem_limit_bytes=16 * MIB),
        name="outer",
    )(edges, sums, part, turned, material, *faces)
    packed = device_sum(packed)
    grid_shape = (count, depth, height, width)
    return pl.pallas_call(
        update_kernel,
        in_specs=[whole(pltpu.SMEM)] + [whole()] * 7,
        out_specs=[whole(pltpu.HBM), whole(pltpu.HBM)],
        out_shape=[jax.ShapeDtypeStruct(grid_shape, F32)] * 2,
        scratch_shapes=[
            pltpu.VMEM((depth + 2, height + 2, count, width), F32),
            pltpu.VMEM((SLOTS, count, STEP, width), F32),
            pltpu.VMEM((SLOTS, count, STEP, width), F32),
            pltpu.SemaphoreType.DMA((SLOTS, 2)),
        ],
        compiler_params=pltpu.CompilerParams(vmem_limit_bytes=20 * MIB),
        name="update",
    )(edges, packed, turned, material, *faces)


def solution(mesh):
    field = P(None, "slab", "pencil", None)
    return jax.shard_map(
        local,
        mesh=mesh,
        in_specs=(field, field, P("slab", "pencil", None), P()),
        out_specs=(field, field),
        check_vma=False,
    )
```

```python
import jax
import jax.numpy as jnp
from jax import lax
from jax.experimental import pallas as pl
from jax.experimental.pallas import tpu as pltpu
from jax.sharding import PartitionSpec as P

F32 = jnp.float32
BF16 = jnp.bfloat16
CELLS = 4194304.0
PITCH = 44
STEP = 40
SLOTS = 2
NT = (((1,), (1,)), ((), ()))
TN = (((0,), (0,)), ((), ()))
MIB = 2**20


def face_kernel(basis, z_first, z_last, y_first, y_last, slab, sems):
    depth, height = basis.shape[1:3]
    slots = slab.shape[0]

    def load(z, slot):
        return pltpu.make_async_copy(basis.at[:, z], slab.at[slot], sems.at[slot])

    for z in range(slots - 1):
        load(z, z).start()

    def step(z, _):
        slot = lax.rem(z, slots)

        @pl.when(z + slots - 1 < depth)
        def _():
            load(z + slots - 1, lax.rem(z + slots - 1, slots)).start()

        load(z, slot).wait()
        y_first[z] = jnp.swapaxes(slab[slot, :, :16, :], 0, 1)[0]
        y_last[z] = jnp.swapaxes(slab[slot, :, height - 16 :, :], 0, 1)[15]

        def whole_plane(face):
            for y in range(0, height, 16):
                face[y : y + 16] = jnp.swapaxes(slab[slot, :, y : y + 16, :], 0, 1)

        pl.when(z == 0)(lambda: whole_plane(z_first))
        pl.when(z == depth - 1)(lambda: whole_plane(z_last))
        return 0

    lax.fori_loop(0, depth, step, 0)


def gram_kernel(
    picked, image, basis, sums, turned, image_slab, basis_slab, rows, image_sems, basis_sems
):
    columns, depth, height, width = image.shape
    count = picked.shape[0]
    total = columns + count
    slots = image_slab.shape[0]

    def loads(z, slot):
        return (
            pltpu.make_async_copy(image.at[:, z], image_slab.at[slot], image_sems.at[slot]),
            pltpu.make_async_copy(basis.at[:, z], basis_slab.at[slot], basis_sems.at[slot]),
        )

    for z in range(slots - 1):
        for copy in loads(z, z):
            copy.start()
    sums[...] = jnp.zeros_like(sums)

    def step(z, _):
        slot = lax.rem(z, slots)

        @pl.when(z + slots - 1 < depth)
        def _():
            for copy in loads(z + slots - 1, lax.rem(z + slots - 1, slots)):
                copy.start()

        for copy in loads(z, slot):
            copy.wait()
        for c in range(columns):
            rows[c * PITCH : c * PITCH + height] = image_slab[slot, c].astype(F32)
        for c in range(count):
            at = (columns + c) * PITCH
            rows[at : at + height] = basis_slab[slot, picked[c]].astype(F32)
        for y in range(0, height, 16):
            turned[z, y : y + 16] = jnp.swapaxes(basis_slab[slot, :, y : y + 16, :], 0, 1)
        both = jnp.concatenate(
            [rows[pl.ds(y, total, stride=PITCH), :].astype(BF16) for y in range(height)], 1
        )
        sums[...] += lax.dot_general(both, both[:columns], NT, preferred_element_type=F32)
        return 0

    lax.fori_loop(0, depth, step, 0)


def coefficient(material):
    squared = jnp.where(
        material == 0, 0.3, jnp.where(material == 1, 0.9, jnp.where(material == 2, 1.6, 2.5))
    ).astype(F32)
    return 6.0 - squared


def beside_in_row(row, first, last):
    width = row.shape[1]
    up = jnp.where(first, 0.0, pltpu.roll(row, 1, 1))
    down = jnp.where(last, 0.0, pltpu.roll(row, width - 1, 1))
    return up + down


def add_plane(gram, scale, below, here, above, before, after, keeps):
    height, columns, width = here.shape
    lane = lax.broadcasted_iota(jnp.int32, (columns, width), 1)
    first, last = lane == 0, lane == width - 1
    middle = [before.astype(F32) * keeps[2], here[0].astype(F32)]
    images = []
    for y in range(height):
        if y == height - 1:
            middle.append(after.astype(F32) * keeps[3])
        else:
            middle.append(here[y + 1].astype(F32))
        row = middle[y + 1]
        under, over = below[y].astype(F32), above[y].astype(F32)
        if keeps[0] is not None:
            under = under * keeps[0]
        if keeps[1] is not None:
            over = over * keeps[1]
        beside = under + over + (middle[y] + middle[y + 2])
        beside = beside + beside_in_row(row, first, last)
        images.append((scale[y : y + 1, :] * row - beside).astype(BF16))
    images = jnp.concatenate(images, 1)
    gram[...] += lax.dot_general(images, images, NT, preferred_element_type=F32)


def inner_kernel(edges, turned, material, y_low, y_high, gram):
    depth = turned.shape[0]
    gram[...] = jnp.zeros_like(gram)
    keeps = (None, None, edges[2].astype(F32), edges[3].astype(F32))

    def step(z, _):
        planes = (turned.at[z - 1], turned.at[z], turned.at[z + 1])
        add_plane(gram, coefficient(material[z]), *planes, y_low[z], y_high[z], keeps)
        return 0

    lax.fori_loop(1, depth - 1, step, 0)


def outer_kernel(
    edges, sums, part, turned, material, z_low, z_high, y_low, y_high, packed, gram
):
    depth, height, columns, width = turned.shape
    count = sums.shape[0] - columns
    gram[...] = part[...]
    inside = [edges[i].astype(F32) for i in range(4)]
    for z, planes, keeps in (
        (0, (z_low, turned.at[0], turned.at[1]), (inside[0], None)),
        (depth - 1, (turned.at[depth - 2], turned.at[depth - 1], z_high), (None, inside[1])),
    ):
        keeps = keeps + (inside[2], inside[3])
        add_plane(gram, coefficient(material[z]), *planes, y_low[z], y_high[z], keeps)
    side = jnp.zeros((columns, 128 - columns), F32)
    normal = jnp.concatenate([gram[...], side], 1)
    col = lax.broadcasted_iota(jnp.int32, (columns, 128), 1)
    line = lax.broadcasted_iota(jnp.int32, (columns, 128), 0)
    diagonal = jnp.sum(jnp.where(line == col, normal, 0.0), axis=1, keepdims=True)
    grams = sums[:columns]
    picked_t = jnp.concatenate(
        [jnp.concatenate([sums[columns:], jnp.zeros((count, 128 - columns), F32)], 1),
         jnp.zeros((128 - count, 128), F32)], 0
    ).T[:columns]
    placed = pltpu.roll(picked_t, columns, 1)
    grams = jnp.concatenate([grams, side], 1)
    out = jnp.where(line >= col, grams, normal)
    out = jnp.where(col >= columns, placed, out)
    packed[...] = jnp.where(col == columns + count, diagonal, out)


def spread(row, lane):
    return jnp.broadcast_to(row[:, lane : lane + 1], row.shape)


def eliminate(blocks, panel, followers):
    base = 8 * panel
    wide = blocks[panel].shape
    rows = [jnp.broadcast_to(blocks[panel][i : i + 1, :], wide) for i in range(8)]
    heads = [[spread(rows[i], base + j) for j in range(8)] for i in range(8)]
    forward, pivots = [], []
    for k in range(8):
        forward.append(rows[k])
        pivots.append(heads[k][k])
        inverse = 1.0 / heads[k][k]
        rows[k] = rows[k] * inverse
        for j in range(k + 1, 8):
            heads[k][j] = heads[k][j] * inverse
        for i in range(8):
            if i == k:
                continue
            factor = heads[i][k]
            rows[i] = rows[i] - factor * rows[k]
            for j in range(k + 1, 8):
                heads[i][j] = heads[i][j] - factor * heads[k][j]
    for i in followers:
        terms = [spread(blocks[i], base + j) * rows[j] for j in range(8)]
        while len(terms) > 1:
            terms = [a + b for a, b in zip(terms[::2], terms[1::2])]
        blocks[i] = blocks[i] - terms[0]
    return rows, forward, pivots


def stacked(rows):
    line = lax.broadcasted_iota(jnp.int32, rows[0].shape, 0)
    out = rows[0]
    for i in range(1, 8):
        out = jnp.where(line == i, rows[i], out)
    return out


def combination(packed, columns, count):
    exact = lax.Precision.HIGHEST
    shape = (128, 128)
    col = lax.broadcasted_iota(jnp.int32, shape, 1)
    line = lax.broadcasted_iota(jnp.int32, shape, 0)
    full = jnp.concatenate([packed, jnp.zeros((128 - columns, 128), F32)], 0)
    flipped = full.T
    grams = jnp.where(line >= col, full, flipped)
    grams = jnp.where(col >= columns, full, grams)
    diagonal = jnp.broadcast_to(full[:, columns + count : columns + count + 1], shape)
    normal = jnp.where(line < col, full, flipped)
    normal = jnp.where(line == col, diagonal, normal)
    normal = jnp.where((col < columns) & (line < columns), normal, 0.0)
    blocks = [grams[8 * i : 8 * i + 8] for i in range(columns // 8)]
    for panel in range(len(blocks)):
        rest = [i for i in range(len(blocks)) if i != panel]
        rows, _, _ = eliminate(blocks, panel, rest)
        blocks[panel] = stacked(rows)
    solved = jnp.concatenate(blocks + [jnp.zeros((128 - columns, 128), F32)], 0)
    solved = pltpu.roll(solved, 128 - columns, 1)
    chosen = jnp.where(col < count, solved, 0.0).astype(BF16).astype(F32)
    chosen_t = chosen.T
    product = jnp.dot(normal, chosen, precision=exact, preferred_element_type=F32)
    normal = jnp.dot(chosen_t, product, precision=exact, preferred_element_type=F32)
    normal = normal[:count] * (1.0 / CELLS)
    joined = jnp.where(col[:count] < count, normal, pltpu.roll(chosen_t[:count], count, 1))
    blocks = [joined[8 * i : 8 * i + 8] for i in range(count // 8)]
    for panel in range(len(blocks)):
        rest = range(panel + 1, len(blocks))
        _, forward, pivots = eliminate(blocks, panel, rest)
        blocks[panel] = stacked([r * lax.rsqrt(d) for r, d in zip(forward, pivots)])
    return pltpu.roll(jnp.concatenate(blocks, 0), 128 - count, 1)[:, :columns]


def update_kernel(
    edges, packed, turned, material, z_low, z_high, y_low, y_high, recycle, images,
    planes, first_out, second_out, store_sems,
):
    depth, height, columns, width = turned.shape
    count = recycle.shape[0]
    weights = combination(packed[...], columns, count)
    rounded = weights.astype(BF16)
    both = jnp.concatenate([rounded, (weights - rounded.astype(F32)).astype(BF16)], 0)

    def combine(row):
        part = jnp.dot(both, row, preferred_element_type=F32)
        return part[:count] + part[count:]

    low = combine(jnp.concatenate([y_low[z] for z in range(depth)], 1))
    high = combine(jnp.concatenate([y_high[z] for z in range(depth)], 1))
    for z in range(depth):
        planes[z + 1, 0] = low[:, z * width : (z + 1) * width] * edges[2].astype(F32)
        planes[z + 1, height + 1] = high[:, z * width : (z + 1) * width] * edges[3].astype(F32)

    def fill(z, source, keep=None):
        plane = combine(jnp.concatenate([source[y] for y in range(height)], 1))
        if keep is not None:
            plane = plane * keep.astype(F32)
        for y in range(height):
            planes[z, y + 1] = plane[:, y * width : (y + 1) * width]

    def stores(z, slot):
        return (
            pltpu.make_async_copy(first_out.at[slot, :, :height], recycle.at[:, z], store_sems.at[slot, 0]),
            pltpu.make_async_copy(second_out.at[slot, :, :height], images.at[:, z], store_sems.at[slot, 1]),
        )

    fill(0, z_low, edges[0])
    fill(1, turned.at[0])
    lane = lax.broadcasted_iota(jnp.int32, (count, width), 1)
    first, last = lane == 0, lane == width - 1

    def step(z, _):
        slot = lax.rem(z, SLOTS)

        @pl.when(z + 1 < depth)
        def _():
            fill(z + 2, turned.at[z + 1])

        @pl.when(z + 1 == depth)
        def _():
            fill(z + 2, z_high, edges[1])

        @pl.when(z >= SLOTS)
        def _():
            for copy in stores(z - SLOTS, slot):
                copy.wait()

        scale = coefficient(material[z])
        one = first_out.at[slot].reshape(count * STEP, width)
        two = second_out.at[slot].reshape(count * STEP, width)
        for y in range(height):
            row = planes[z + 1, y + 1]
            beside = planes[z, y + 1] + planes[z + 2, y + 1]
            beside = beside + (planes[z + 1, y] + planes[z + 1, y + 2])
            beside = beside + beside_in_row(row, first, last)
            one[pl.ds(y, count, stride=STEP), :] = row
            two[pl.ds(y, count, stride=STEP), :] = scale[y : y + 1, :] * row - beside
        for copy in stores(z, slot):
            copy.start()
        return 0

    lax.fori_loop(0, depth, step, 0)
    for z in range(depth - SLOTS, depth):
        for copy in stores(z, z % SLOTS):
            copy.wait()


def device_sum(value):
    def exchanged(axis, size, distance):
        return lax.ppermute(value, axis, [(i, i ^ distance) for i in range(size)])

    value = value + exchanged("slab", 32, 1)
    for axis, size, stride in (("slab", 32, 8), ("slab", 32, 2), ("pencil", 4, 1)):
        near, opposite, far = [exchanged(axis, size, d * stride) for d in (1, 2, 3)]
        value = (value + opposite) + (near + far)
    return value


def whole(memory=pltpu.VMEM):
    return pl.BlockSpec(memory_space=memory)


def local(basis, image, material, picked):
    columns, depth, height, width = basis.shape
    count = picked.shape[0]
    slabs, pencils = lax.axis_size("slab"), lax.axis_size("pencil")

    def neighbours(low_face, high_face, axis, size):
        up = [(i, (i + 1) % size) for i in range(size)]
        down = [(j, i) for i, j in up]
        return lax.ppermute(high_face, axis, up), lax.ppermute(low_face, axis, down)

    face = jax.ShapeDtypeStruct((height, columns, width), BF16)
    edge = jax.ShapeDtypeStruct((depth, columns, width), BF16)
    z_first, z_last, y_first, y_last = pl.pallas_call(
        face_kernel,
        in_specs=[whole(pltpu.HBM)],
        out_specs=[whole()] * 4,
        out_shape=[face, face, edge, edge],
        scratch_shapes=[
            pltpu.VMEM((4, columns, height, width), BF16),
            pltpu.SemaphoreType.DMA((4,)),
        ],
        compiler_params=pltpu.CompilerParams(vmem_limit_bytes=52 * MIB),
        name="faces",
    )(basis)
    z_low, z_high = neighbours(z_first, z_last, "slab", slabs)
    y_low, y_high = neighbours(y_first, y_last, "pencil", pencils)
    sums, turned = pl.pallas_call(
        gram_kernel,
        in_specs=[whole(pltpu.SMEM), whole(pltpu.HBM), whole(pltpu.HBM)],
        out_specs=[whole()] * 2,
        out_shape=[
            jax.ShapeDtypeStruct((columns + count, columns), F32),
            jax.ShapeDtypeStruct((depth, height, columns, width), BF16),
        ],
        scratch_shapes=[
            pltpu.VMEM((4, columns, height, width), BF16),
            pltpu.VMEM((4, columns, height, width), BF16),
            pltpu.VMEM(((columns + count) * PITCH, width), F32),
            pltpu.SemaphoreType.DMA((4,)),
            pltpu.SemaphoreType.DMA((4,)),
        ],
        compiler_params=pltpu.CompilerParams(vmem_limit_bytes=46 * MIB),
        cost_estimate=pl.CostEstimate(flops=2 * 10**9, bytes_accessed=17 * 10**6, transcendentals=0),
        name="gram",
    )(picked, image, basis)
    faces = (z_low, z_high, y_low, y_high)
    slab, pencil = lax.axis_index("slab"), lax.axis_index("pencil")
    inner = (slab > 0, slab < slabs - 1, pencil > 0, pencil < pencils - 1)
    edges = jnp.stack(inner).astype(jnp.int32)
    grams = jax.ShapeDtypeStruct((columns, columns), F32)
    part = pl.pallas_call(
        inner_kernel,
        in_specs=[whole(pltpu.SMEM)] + [whole()] * 4,
        out_specs=whole(),
        out_shape=grams,
        compiler_params=pltpu.CompilerParams(vmem_limit_bytes=16 * MIB),
        cost_estimate=pl.CostEstimate(flops=10**10, bytes_accessed=10**7, transcendentals=0),
        name="inner",
    )(edges, turned, material, y_low, y_high)
    packed = pl.pallas_call(
        outer_kernel,
        in_specs=[whole(pltpu.SMEM)] + [whole()] * 8,
        out_specs=whole(),
        out_shape=jax.ShapeDtypeStruct((columns, 128), F32),
        scratch_shapes=[pltpu.VMEM(grams.shape, F32)],
        compiler_params=pltpu.CompilerParams(vmem_limit_bytes=16 * MIB),
        name="outer",
    )(edges, sums, part, turned, material, *faces)
    packed = device_sum(packed)
    grid_shape = (count, depth, height, width)
    return pl.pallas_call(
        update_kernel,
        in_specs=[whole(pltpu.SMEM)] + [whole()] * 7,
        out_specs=[whole(pltpu.HBM), whole(pltpu.HBM)],
        out_shape=[jax.ShapeDtypeStruct(grid_shape, F32)] * 2,
        scratch_shapes=[
            pltpu.VMEM((depth + 2, height + 2, count, width), F32),
            pltpu.VMEM((SLOTS, count, STEP, width), F32),
            pltpu.VMEM((SLOTS, count, STEP, width), F32),
            pltpu.SemaphoreType.DMA((SLOTS, 2)),
        ],
        compiler_params=pltpu.CompilerParams(vmem_limit_bytes=20 * MIB),
        name="update",
    )(edges, packed, turned, material, *faces)


def solution(mesh):
    field = P(None, "slab", "pencil", None)
    return jax.shard_map(
        local,
        mesh=mesh,
        in_specs=(field, field, P("slab", "pencil", None), P()),
        out_specs=(field, field),
        check_vma=False,
    )
```

```python
import jax
import jax.numpy as jnp
from jax import lax
from jax.experimental import pallas as pl
from jax.experimental.pallas import tpu as pltpu
from jax.sharding import PartitionSpec as P

F32 = jnp.float32
BF16 = jnp.bfloat16
CELLS = 4194304.0
PITCH = 44
STEP = 40
SLOTS = 2
NT = (((1,), (1,)), ((), ()))
TN = (((0,), (0,)), ((), ()))
MIB = 2**20


def face_kernel(basis, z_first, z_last, y_first, y_last, slab, sems):
    depth, height = basis.shape[1:3]
    slots = slab.shape[0]

    def load(z, slot):
        return pltpu.make_async_copy(basis.at[:, z], slab.at[slot], sems.at[slot])

    for z in range(slots - 1):
        load(z, z).start()

    def step(z, _):
        slot = lax.rem(z, slots)

        @pl.when(z + slots - 1 < depth)
        def _():
            load(z + slots - 1, lax.rem(z + slots - 1, slots)).start()

        load(z, slot).wait()
        y_first[z] = jnp.swapaxes(slab[slot, :, :16, :], 0, 1)[0]
        y_last[z] = jnp.swapaxes(slab[slot, :, height - 16 :, :], 0, 1)[15]

        def whole_plane(face):
            for y in range(0, height, 16):
                face[y : y + 16] = jnp.swapaxes(slab[slot, :, y : y + 16, :], 0, 1)

        pl.when(z == 0)(lambda: whole_plane(z_first))
        pl.when(z == depth - 1)(lambda: whole_plane(z_last))
        return 0

    lax.fori_loop(0, depth, step, 0)


def gram_kernel(
    picked, image, basis, sums, turned, image_slab, basis_slab, rows, image_sems, basis_sems
):
    columns, depth, height, width = image.shape
    count = picked.shape[0]
    total = columns + count
    slots = image_slab.shape[0]

    def loads(z, slot):
        return (
            pltpu.make_async_copy(image.at[:, z], image_slab.at[slot], image_sems.at[slot]),
            pltpu.make_async_copy(basis.at[:, z], basis_slab.at[slot], basis_sems.at[slot]),
        )

    for z in range(slots - 1):
        for copy in loads(z, z):
            copy.start()
    sums[...] = jnp.zeros_like(sums)

    def step(z, _):
        slot = lax.rem(z, slots)

        @pl.when(z + slots - 1 < depth)
        def _():
            for copy in loads(z + slots - 1, lax.rem(z + slots - 1, slots)):
                copy.start()

        for copy in loads(z, slot):
            copy.wait()
        for c in range(columns):
            rows[c * PITCH : c * PITCH + height] = image_slab[slot, c].astype(F32)
        for c in range(count):
            at = (columns + c) * PITCH
            rows[at : at + height] = basis_slab[slot, picked[c]].astype(F32)
        for y in range(0, height, 16):
            turned[z, y : y + 16] = jnp.swapaxes(basis_slab[slot, :, y : y + 16, :], 0, 1)
        both = jnp.concatenate(
            [rows[pl.ds(y, total, stride=PITCH), :].astype(BF16) for y in range(height)], 1
        )
        sums[...] += lax.dot_general(both, both[:columns], NT, preferred_element_type=F32)
        return 0

    lax.fori_loop(0, depth, step, 0)


def coefficient(material):
    squared = jnp.where(
        material == 0, 0.3, jnp.where(material == 1, 0.9, jnp.where(material == 2, 1.6, 2.5))
    ).astype(F32)
    return 6.0 - squared


def beside_in_row(row, first, last):
    width = row.shape[1]
    up = jnp.where(first, 0.0, pltpu.roll(row, 1, 1))
    down = jnp.where(last, 0.0, pltpu.roll(row, width - 1, 1))
    return up + down


def add_plane(gram, scale, below, here, above, before, after, keeps):
    height, columns, width = here.shape
    lane = lax.broadcasted_iota(jnp.int32, (columns, width), 1)
    first, last = lane == 0, lane == width - 1
    middle = [before.astype(F32) * keeps[2], here[0].astype(F32)]
    images = []
    for y in range(height):
        if y == height - 1:
            middle.append(after.astype(F32) * keeps[3])
        else:
            middle.append(here[y + 1].astype(F32))
        row = middle[y + 1]
        under, over = below[y].astype(F32), above[y].astype(F32)
        if keeps[0] is not None:
            under = under * keeps[0]
        if keeps[1] is not None:
            over = over * keeps[1]
        beside = under + over + (middle[y] + middle[y + 2])
        beside = beside + beside_in_row(row, first, last)
        images.append((scale[y : y + 1, :] * row - beside).astype(BF16))
    images = jnp.concatenate(images, 1)
    gram[...] += lax.dot_general(images, images, NT, preferred_element_type=F32)


def inner_kernel(edges, turned, material, y_low, y_high, gram):
    depth = turned.shape[0]
    gram[...] = jnp.zeros_like(gram)
    keeps = (None, None, edges[2].astype(F32), edges[3].astype(F32))

    def step(z, _):
        planes = (turned.at[z - 1], turned.at[z], turned.at[z + 1])
        add_plane(gram, coefficient(material[z]), *planes, y_low[z], y_high[z], keeps)
        return 0

    lax.fori_loop(1, depth - 1, step, 0)


def outer_kernel(
    edges, sums, part, turned, material, z_low, z_high, y_low, y_high, packed, gram
):
    depth, height, columns, width = turned.shape
    count = sums.shape[0] - columns
    gram[...] = part[...]
    inside = [edges[i].astype(F32) for i in range(4)]
    for z, planes, keeps in (
        (0, (z_low, turned.at[0], turned.at[1]), (inside[0], None)),
        (depth - 1, (turned.at[depth - 2], turned.at[depth - 1], z_high), (None, inside[1])),
    ):
        keeps = keeps + (inside[2], inside[3])
        add_plane(gram, coefficient(material[z]), *planes, y_low[z], y_high[z], keeps)
    side = jnp.zeros((columns, 128 - columns), F32)
    normal = jnp.concatenate([gram[...], side], 1)
    col = lax.broadcasted_iota(jnp.int32, (columns, 128), 1)
    line = lax.broadcasted_iota(jnp.int32, (columns, 128), 0)
    diagonal = jnp.sum(jnp.where(line == col, normal, 0.0), axis=1, keepdims=True)
    grams = sums[:columns]
    picked_t = jnp.concatenate(
        [jnp.concatenate([sums[columns:], jnp.zeros((count, 128 - columns), F32)], 1),
         jnp.zeros((128 - count, 128), F32)], 0
    ).T[:columns]
    placed = pltpu.roll(picked_t, columns, 1)
    grams = jnp.concatenate([grams, side], 1)
    out = jnp.where(line >= col, grams, normal)
    out = jnp.where(col >= columns, placed, out)
    packed[...] = jnp.where(col == columns + count, diagonal, out)


def spread(row, lane):
    return jnp.broadcast_to(row[:, lane : lane + 1], row.shape)


def eliminate(blocks, panel, followers):
    base = 8 * panel
    wide = blocks[panel].shape
    rows = [jnp.broadcast_to(blocks[panel][i : i + 1, :], wide) for i in range(8)]
    heads = [[spread(rows[i], base + j) for j in range(8)] for i in range(8)]
    forward, pivots = [], []
    for k in range(8):
        forward.append(rows[k])
        pivots.append(heads[k][k])
        inverse = 1.0 / heads[k][k]
        rows[k] = rows[k] * inverse
        for j in range(k + 1, 8):
            heads[k][j] = heads[k][j] * inverse
        for i in range(8):
            if i == k:
                continue
            factor = heads[i][k]
            rows[i] = rows[i] - factor * rows[k]
            for j in range(k + 1, 8):
                heads[i][j] = heads[i][j] - factor * heads[k][j]
    for i in followers:
        terms = [spread(blocks[i], base + j) * rows[j] for j in range(8)]
        while len(terms) > 1:
            terms = [a + b for a, b in zip(terms[::2], terms[1::2])]
        blocks[i] = blocks[i] - terms[0]
    return rows, forward, pivots


def stacked(rows):
    line = lax.broadcasted_iota(jnp.int32, rows[0].shape, 0)
    out = rows[0]
    for i in range(1, 8):
        out = jnp.where(line == i, rows[i], out)
    return out


def parts(value):
    out = []
    for _ in range(3):
        out.append(value.astype(BF16))
        value = value - out[-1].astype(F32)
    return out


def combination(packed, columns, count):
    shape = (128, 128)
    col = lax.broadcasted_iota(jnp.int32, shape, 1)
    line = lax.broadcasted_iota(jnp.int32, shape, 0)
    full = jnp.concatenate([packed, jnp.zeros((128 - columns, 128), F32)], 0)
    flipped = full.T
    grams = jnp.where(line >= col, full, flipped)
    grams = jnp.where(col >= columns, full, grams)
    diagonal = jnp.broadcast_to(full[:, columns + count : columns + count + 1], shape)
    normal = jnp.where(line < col, full, flipped)
    normal = jnp.where(line == col, diagonal, normal)
    normal = jnp.where((col < columns) & (line < columns), normal, 0.0)
    blocks = [grams[8 * i : 8 * i + 8] for i in range(columns // 8)]
    for panel in range(len(blocks)):
        rest = [i for i in range(len(blocks)) if i != panel]
        rows, _, _ = eliminate(blocks, panel, rest)
        blocks[panel] = stacked(rows)
    solved = jnp.concatenate(blocks + [jnp.zeros((128 - columns, 128), F32)], 0)
    solved = pltpu.roll(solved, 128 - columns, 1)
    chosen = jnp.where(col < count, solved, 0.0).astype(BF16)
    chosen_t = chosen.astype(F32).T
    product = jnp.dot(jnp.concatenate(parts(normal), 0), chosen, preferred_element_type=F32)
    product = product[:128] + (product[128:256] + product[256:])
    short_t = chosen_t[:count].astype(BF16)
    normal = jnp.dot(short_t, jnp.concatenate(parts(product), 1), preferred_element_type=F32)
    normal = normal[:, :128] + (normal[:, 128:256] + normal[:, 256:])
    normal = normal * (1.0 / CELLS)
    joined = jnp.where(col[:count] < count, normal, pltpu.roll(chosen_t[:count], count, 1))
    blocks = [joined[8 * i : 8 * i + 8] for i in range(count // 8)]
    for panel in range(len(blocks)):
        rest = range(panel + 1, len(blocks))
        _, forward, pivots = eliminate(blocks, panel, rest)
        blocks[panel] = stacked([r * lax.rsqrt(d) for r, d in zip(forward, pivots)])
    return pltpu.roll(jnp.concatenate(blocks, 0), 128 - count, 1)[:, :columns]


def update_kernel(
    edges, packed, turned, material, z_low, z_high, y_low, y_high, recycle, images,
    planes, first_out, second_out, store_sems,
):
    depth, height, columns, width = turned.shape
    count = recycle.shape[0]
    weights = combination(packed[...], columns, count)
    rounded = weights.astype(BF16)
    both = jnp.concatenate([rounded, (weights - rounded.astype(F32)).astype(BF16)], 0)

    def combine(row):
        part = jnp.dot(both, row, preferred_element_type=F32)
        return part[:count] + part[count:]

    low = combine(jnp.concatenate([y_low[z] for z in range(depth)], 1))
    high = combine(jnp.concatenate([y_high[z] for z in range(depth)], 1))
    for z in range(depth):
        planes[z + 1, 0] = low[:, z * width : (z + 1) * width] * edges[2].astype(F32)
        planes[z + 1, height + 1] = high[:, z * width : (z + 1) * width] * edges[3].astype(F32)

    def fill(z, source, keep=None):
        plane = combine(jnp.concatenate([source[y] for y in range(height)], 1))
        if keep is not None:
            plane = plane * keep.astype(F32)
        for y in range(height):
            planes[z, y + 1] = plane[:, y * width : (y + 1) * width]

    def stores(z, slot):
        return (
            pltpu.make_async_copy(first_out.at[slot, :, :height], recycle.at[:, z], store_sems.at[slot, 0]),
            pltpu.make_async_copy(second_out.at[slot, :, :height], images.at[:, z], store_sems.at[slot, 1]),
        )

    fill(0, z_low, edges[0])
    fill(1, turned.at[0])
    fill(2, turned.at[1])
    lane = lax.broadcasted_iota(jnp.int32, (count, width), 1)
    first, last = lane == 0, lane == width - 1

    def write(z, ahead):
        slot = lax.rem(z, SLOTS)

        @pl.when(z >= SLOTS)
        def _():
            for copy in stores(z - SLOTS, slot):
                copy.wait()

        scale = coefficient(material[z])
        one = first_out.at[slot].reshape(count * STEP, width)
        two = second_out.at[slot].reshape(count * STEP, width)
        if ahead:
            fill(z + 3, turned.at[z + 2])
        for y in range(height):
            row = planes[z + 1, y + 1]
            beside = planes[z, y + 1] + planes[z + 2, y + 1]
            beside = beside + (planes[z + 1, y] + planes[z + 1, y + 2])
            beside = beside + beside_in_row(row, first, last)
            one[pl.ds(y, count, stride=STEP), :] = row
            two[pl.ds(y, count, stride=STEP), :] = scale[y : y + 1, :] * row - beside
        for copy in stores(z, slot):
            copy.start()
        return 0

    lax.fori_loop(0, depth - 2, lambda z, _: write(z, True), 0)
    fill(depth + 1, z_high, edges[1])
    lax.fori_loop(depth - 2, depth, lambda z, _: write(z, False), 0)
    for z in range(depth - SLOTS, depth):
        for copy in stores(z, z % SLOTS):
            copy.wait()


def device_sum(value):
    def exchanged(axis, size, distance):
        return lax.ppermute(value, axis, [(i, i ^ distance) for i in range(size)])

    value = value + exchanged("slab", 32, 1)
    for axis, size, stride in (("slab", 32, 8), ("slab", 32, 2), ("pencil", 4, 1)):
        near, opposite, far = [exchanged(axis, size, d * stride) for d in (1, 2, 3)]
        value = (value + opposite) + (near + far)
    return value


def whole(memory=pltpu.VMEM):
    return pl.BlockSpec(memory_space=memory)


def local(basis, image, material, picked):
    columns, depth, height, width = basis.shape
    count = picked.shape[0]
    slabs, pencils = lax.axis_size("slab"), lax.axis_size("pencil")

    def neighbours(low_face, high_face, axis, size):
        up = [(i, (i + 1) % size) for i in range(size)]
        down = [(j, i) for i, j in up]
        return lax.ppermute(high_face, axis, up), lax.ppermute(low_face, axis, down)

    face = jax.ShapeDtypeStruct((height, columns, width), BF16)
    edge = jax.ShapeDtypeStruct((depth, columns, width), BF16)
    z_first, z_last, y_first, y_last = pl.pallas_call(
        face_kernel,
        in_specs=[whole(pltpu.HBM)],
        out_specs=[whole()] * 4,
        out_shape=[face, face, edge, edge],
        scratch_shapes=[
            pltpu.VMEM((4, columns, height, width), BF16),
            pltpu.SemaphoreType.DMA((4,)),
        ],
        compiler_params=pltpu.CompilerParams(vmem_limit_bytes=52 * MIB),
        name="faces",
    )(basis)
    z_low, z_high = neighbours(z_first, z_last, "slab", slabs)
    y_low, y_high = neighbours(y_first, y_last, "pencil", pencils)
    sums, turned = pl.pallas_call(
        gram_kernel,
        in_specs=[whole(pltpu.SMEM), whole(pltpu.HBM), whole(pltpu.HBM)],
        out_specs=[whole()] * 2,
        out_shape=[
            jax.ShapeDtypeStruct((columns + count, columns), F32),
            jax.ShapeDtypeStruct((depth, height, columns, width), BF16),
        ],
        scratch_shapes=[
            pltpu.VMEM((4, columns, height, width), BF16),
            pltpu.VMEM((4, columns, height, width), BF16),
            pltpu.VMEM(((columns + count) * PITCH, width), F32),
            pltpu.SemaphoreType.DMA((4,)),
            pltpu.SemaphoreType.DMA((4,)),
        ],
        compiler_params=pltpu.CompilerParams(vmem_limit_bytes=46 * MIB),
        cost_estimate=pl.CostEstimate(flops=2 * 10**9, bytes_accessed=17 * 10**6, transcendentals=0),
        name="gram",
    )(picked, image, basis)
    faces = (z_low, z_high, y_low, y_high)
    slab, pencil = lax.axis_index("slab"), lax.axis_index("pencil")
    inner = (slab > 0, slab < slabs - 1, pencil > 0, pencil < pencils - 1)
    edges = jnp.stack(inner).astype(jnp.int32)
    grams = jax.ShapeDtypeStruct((columns, columns), F32)
    part = pl.pallas_call(
        inner_kernel,
        in_specs=[whole(pltpu.SMEM)] + [whole()] * 4,
        out_specs=whole(),
        out_shape=grams,
        compiler_params=pltpu.CompilerParams(vmem_limit_bytes=16 * MIB),
        cost_estimate=pl.CostEstimate(flops=10**10, bytes_accessed=10**7, transcendentals=0),
        name="inner",
    )(edges, turned, material, y_low, y_high)
    packed = pl.pallas_call(
        outer_kernel,
        in_specs=[whole(pltpu.SMEM)] + [whole()] * 8,
        out_specs=whole(),
        out_shape=jax.ShapeDtypeStruct((columns, 128), F32),
        scratch_shapes=[pltpu.VMEM(grams.shape, F32)],
        compiler_params=pltpu.CompilerParams(vmem_limit_bytes=16 * MIB),
        name="outer",
    )(edges, sums, part, turned, material, *faces)
    packed = device_sum(packed)
    grid_shape = (count, depth, height, width)
    return pl.pallas_call(
        update_kernel,
        in_specs=[whole(pltpu.SMEM)] + [whole()] * 7,
        out_specs=[whole(pltpu.HBM), whole(pltpu.HBM)],
        out_shape=[jax.ShapeDtypeStruct(grid_shape, F32)] * 2,
        scratch_shapes=[
            pltpu.VMEM((depth + 2, height + 2, count, width), F32),
            pltpu.VMEM((SLOTS, count, STEP, width), F32),
            pltpu.VMEM((SLOTS, count, STEP, width), F32),
            pltpu.SemaphoreType.DMA((SLOTS, 2)),
        ],
        compiler_params=pltpu.CompilerParams(vmem_limit_bytes=20 * MIB),
        name="update",
    )(edges, packed, turned, material, *faces)


def solution(mesh):
    field = P(None, "slab", "pencil", None)
    return jax.shard_map(
        local,
        mesh=mesh,
        in_specs=(field, field, P("slab", "pencil", None), P()),
        out_specs=(field, field),
        check_vma=False,
    )
```

```python
import jax
import jax.numpy as jnp
from jax import lax
from jax.experimental import pallas as pl
from jax.experimental.pallas import tpu as pltpu
from jax.sharding import PartitionSpec as P

F32 = jnp.float32
BF16 = jnp.bfloat16
CELLS = 4194304.0
PITCH = 44
STEP = 40
SLOTS = 2
NT = (((1,), (1,)), ((), ()))
TN = (((0,), (0,)), ((), ()))
MIB = 2**20


def face_kernel(basis, z_first, z_last, y_first, y_last, slab, sems):
    depth, height = basis.shape[1:3]

    def load(i):
        z = lax.rem(depth - i, depth)
        return pltpu.make_async_copy(basis.at[:, z], slab.at[i], sems.at[i])

    for i in range(depth):
        load(i).start()

    def step(i, _):
        z = lax.rem(depth - i, depth)
        load(i).wait()
        y_first[z] = jnp.swapaxes(slab[i, :, :16, :], 0, 1)[0]
        y_last[z] = jnp.swapaxes(slab[i, :, height - 16 :, :], 0, 1)[15]

        def whole_plane(face):
            for y in range(0, height, 16):
                face[y : y + 16] = jnp.swapaxes(slab[i, :, y : y + 16, :], 0, 1)

        pl.when(z == 0)(lambda: whole_plane(z_first))
        pl.when(z == depth - 1)(lambda: whole_plane(z_last))
        return 0

    lax.fori_loop(0, depth, step, 0)


def gram_kernel(
    picked, image, basis, sums, turned, image_slab, basis_slab, rows, image_sems, basis_sems
):
    columns, depth, height, width = image.shape
    count = picked.shape[0]
    total = columns + count
    slots = image_slab.shape[0]

    def loads(z, slot):
        return (
            pltpu.make_async_copy(image.at[:, z], image_slab.at[slot], image_sems.at[slot]),
            pltpu.make_async_copy(basis.at[:, z], basis_slab.at[slot], basis_sems.at[slot]),
        )

    for z in range(slots - 1):
        for copy in loads(z, z):
            copy.start()
    sums[...] = jnp.zeros_like(sums)

    def step(z, _):
        slot = lax.rem(z, slots)

        @pl.when(z + slots - 1 < depth)
        def _():
            for copy in loads(z + slots - 1, lax.rem(z + slots - 1, slots)):
                copy.start()

        for copy in loads(z, slot):
            copy.wait()
        for c in range(columns):
            rows[c * PITCH : c * PITCH + height] = image_slab[slot, c].astype(F32)
        for c in range(count):
            at = (columns + c) * PITCH
            rows[at : at + height] = basis_slab[slot, picked[c]].astype(F32)
        for y in range(0, height, 16):
            turned[z, y : y + 16] = jnp.swapaxes(basis_slab[slot, :, y : y + 16, :], 0, 1)
        both = jnp.concatenate(
            [rows[pl.ds(y, total, stride=PITCH), :].astype(BF16) for y in range(height)], 1
        )
        sums[...] += lax.dot_general(both, both[:columns], NT, preferred_element_type=F32)
        return 0

    lax.fori_loop(0, depth, step, 0)


def coefficient(material):
    squared = jnp.where(
        material == 0, 0.3, jnp.where(material == 1, 0.9, jnp.where(material == 2, 1.6, 2.5))
    ).astype(F32)
    return 6.0 - squared


def beside_in_row(row, first, last):
    width = row.shape[1]
    up = jnp.where(first, 0.0, pltpu.roll(row, 1, 1))
    down = jnp.where(last, 0.0, pltpu.roll(row, width - 1, 1))
    return up + down


def add_plane(gram, scale, below, here, above, before, after, keeps):
    height, columns, width = here.shape
    lane = lax.broadcasted_iota(jnp.int32, (columns, width), 1)
    first, last = lane == 0, lane == width - 1
    middle = [before.astype(F32) * keeps[2], here[0].astype(F32)]
    images = []
    for y in range(height):
        if y == height - 1:
            middle.append(after.astype(F32) * keeps[3])
        else:
            middle.append(here[y + 1].astype(F32))
        row = middle[y + 1]
        under, over = below[y].astype(F32), above[y].astype(F32)
        if keeps[0] is not None:
            under = under * keeps[0]
        if keeps[1] is not None:
            over = over * keeps[1]
        beside = under + over + (middle[y] + middle[y + 2])
        beside = beside + beside_in_row(row, first, last)
        images.append((scale[y : y + 1, :] * row - beside).astype(BF16))
    images = jnp.concatenate(images, 1)
    gram[...] += lax.dot_general(images, images, NT, preferred_element_type=F32)


def inner_kernel(edges, turned, material, y_low, y_high, gram):
    depth = turned.shape[0]
    gram[...] = jnp.zeros_like(gram)
    keeps = (None, None, edges[2].astype(F32), edges[3].astype(F32))

    def step(z, _):
        planes = (turned.at[z - 1], turned.at[z], turned.at[z + 1])
        add_plane(gram, coefficient(material[z]), *planes, y_low[z], y_high[z], keeps)
        return 0

    lax.fori_loop(1, depth - 1, step, 0)


def outer_kernel(
    edges, sums, part, turned, material, z_low, z_high, y_low, y_high, packed, gram
):
    depth, height, columns, width = turned.shape
    count = sums.shape[0] - columns
    gram[...] = part[...]
    inside = [edges[i].astype(F32) for i in range(4)]
    for z, planes, keeps in (
        (0, (z_low, turned.at[0], turned.at[1]), (inside[0], None)),
        (depth - 1, (turned.at[depth - 2], turned.at[depth - 1], z_high), (None, inside[1])),
    ):
        keeps = keeps + (inside[2], inside[3])
        add_plane(gram, coefficient(material[z]), *planes, y_low[z], y_high[z], keeps)
    side = jnp.zeros((columns, 128 - columns), F32)
    normal = jnp.concatenate([gram[...], side], 1)
    col = lax.broadcasted_iota(jnp.int32, (columns, 128), 1)
    line = lax.broadcasted_iota(jnp.int32, (columns, 128), 0)
    diagonal = jnp.sum(jnp.where(line == col, normal, 0.0), axis=1, keepdims=True)
    grams = sums[:columns]
    picked_t = jnp.concatenate(
        [jnp.concatenate([sums[columns:], jnp.zeros((count, 128 - columns), F32)], 1),
         jnp.zeros((128 - count, 128), F32)], 0
    ).T[:columns]
    placed = pltpu.roll(picked_t, columns, 1)
    grams = jnp.concatenate([grams, side], 1)
    out = jnp.where(line >= col, grams, normal)
    out = jnp.where(col >= columns, placed, out)
    packed[...] = jnp.where(col == columns + count, diagonal, out)


def spread(row, lane):
    return jnp.broadcast_to(row[:, lane : lane + 1], row.shape)


def eliminate(blocks, panel, followers):
    base = 8 * panel
    wide = blocks[panel].shape
    rows = [jnp.broadcast_to(blocks[panel][i : i + 1, :], wide) for i in range(8)]
    heads = [[spread(rows[i], base + j) for j in range(8)] for i in range(8)]
    forward, pivots = [], []
    for k in range(8):
        forward.append(rows[k])
        pivots.append(heads[k][k])
        inverse = 1.0 / heads[k][k]
        rows[k] = rows[k] * inverse
        for j in range(k + 1, 8):
            heads[k][j] = heads[k][j] * inverse
        for i in range(8):
            if i == k:
                continue
            factor = heads[i][k]
            rows[i] = rows[i] - factor * rows[k]
            for j in range(k + 1, 8):
                heads[i][j] = heads[i][j] - factor * heads[k][j]
    for i in followers:
        terms = [spread(blocks[i], base + j) * rows[j] for j in range(8)]
        while len(terms) > 1:
            terms = [a + b for a, b in zip(terms[::2], terms[1::2])]
        blocks[i] = blocks[i] - terms[0]
    return rows, forward, pivots


def stacked(rows):
    line = lax.broadcasted_iota(jnp.int32, rows[0].shape, 0)
    out = rows[0]
    for i in range(1, 8):
        out = jnp.where(line == i, rows[i], out)
    return out


def parts(value):
    out = []
    for _ in range(3):
        out.append(value.astype(BF16))
        value = value - out[-1].astype(F32)
    return out


def combination(packed, columns, count):
    shape = (128, 128)
    col = lax.broadcasted_iota(jnp.int32, shape, 1)
    line = lax.broadcasted_iota(jnp.int32, shape, 0)
    full = jnp.concatenate([packed, jnp.zeros((128 - columns, 128), F32)], 0)
    flipped = full.T
    grams = jnp.where(line >= col, full, flipped)
    grams = jnp.where(col >= columns, full, grams)
    diagonal = jnp.broadcast_to(full[:, columns + count : columns + count + 1], shape)
    normal = jnp.where(line < col, full, flipped)
    normal = jnp.where(line == col, diagonal, normal)
    normal = jnp.where((col < columns) & (line < columns), normal, 0.0)
    blocks = [grams[8 * i : 8 * i + 8] for i in range(columns // 8)]
    for panel in range(len(blocks)):
        rest = [i for i in range(len(blocks)) if i != panel]
        rows, _, _ = eliminate(blocks, panel, rest)
        blocks[panel] = stacked(rows)
    solved = jnp.concatenate(blocks + [jnp.zeros((128 - columns, 128), F32)], 0)
    solved = pltpu.roll(solved, 128 - columns, 1)
    chosen = jnp.where(col < count, solved, 0.0).astype(BF16)
    chosen_t = chosen.astype(F32).T
    product = jnp.dot(jnp.concatenate(parts(normal), 0), chosen, preferred_element_type=F32)
    product = product[:128] + (product[128:256] + product[256:])
    short_t = chosen_t[:count].astype(BF16)
    normal = jnp.dot(short_t, jnp.concatenate(parts(product), 1), preferred_element_type=F32)
    normal = normal[:, :128] + (normal[:, 128:256] + normal[:, 256:])
    normal = normal * (1.0 / CELLS)
    joined = jnp.where(col[:count] < count, normal, pltpu.roll(chosen_t[:count], count, 1))
    blocks = [joined[8 * i : 8 * i + 8] for i in range(count // 8)]
    for panel in range(len(blocks)):
        rest = range(panel + 1, len(blocks))
        _, forward, pivots = eliminate(blocks, panel, rest)
        blocks[panel] = stacked([r * lax.rsqrt(d) for r, d in zip(forward, pivots)])
    return pltpu.roll(jnp.concatenate(blocks, 0), 128 - count, 1)[:, :columns]


def update_kernel(
    edges, packed, turned, material, z_low, z_high, y_low, y_high, recycle, images,
    planes, first_out, second_out, store_sems,
):
    depth, height, columns, width = turned.shape
    count = recycle.shape[0]
    weights = combination(packed[...], columns, count)
    rounded = weights.astype(BF16)
    both = jnp.concatenate([rounded, (weights - rounded.astype(F32)).astype(BF16)], 0)

    def combine(row):
        part = jnp.dot(both, row, preferred_element_type=F32)
        return part[:count] + part[count:]

    low = combine(jnp.concatenate([y_low[z] for z in range(depth)], 1))
    high = combine(jnp.concatenate([y_high[z] for z in range(depth)], 1))
    for z in range(depth):
        planes[z + 1, 0] = low[:, z * width : (z + 1) * width] * edges[2].astype(F32)
        planes[z + 1, height + 1] = high[:, z * width : (z + 1) * width] * edges[3].astype(F32)

    def fill(z, source, keep=None):
        plane = combine(jnp.concatenate([source[y] for y in range(height)], 1))
        if keep is not None:
            plane = plane * keep.astype(F32)
        for y in range(height):
            planes[z, y + 1] = plane[:, y * width : (y + 1) * width]

    def stores(z, slot):
        return (
            pltpu.make_async_copy(first_out.at[slot, :, :height], recycle.at[:, z], store_sems.at[slot, 0]),
            pltpu.make_async_copy(second_out.at[slot, :, :height], images.at[:, z], store_sems.at[slot, 1]),
        )

    fill(0, z_low, edges[0])
    fill(1, turned.at[0])
    fill(2, turned.at[1])
    lane = lax.broadcasted_iota(jnp.int32, (count, width), 1)
    first, last = lane == 0, lane == width - 1

    def write(z, ahead):
        slot = lax.rem(z, SLOTS)

        @pl.when(z >= SLOTS)
        def _():
            for copy in stores(z - SLOTS, slot):
                copy.wait()

        scale = coefficient(material[z])
        one = first_out.at[slot].reshape(count * STEP, width)
        two = second_out.at[slot].reshape(count * STEP, width)
        if ahead:
            fill(z + 3, turned.at[z + 2])
        for y in range(height):
            row = planes[z + 1, y + 1]
            beside = planes[z, y + 1] + planes[z + 2, y + 1]
            beside = beside + (planes[z + 1, y] + planes[z + 1, y + 2])
            beside = beside + beside_in_row(row, first, last)
            one[pl.ds(y, count, stride=STEP), :] = row
            two[pl.ds(y, count, stride=STEP), :] = scale[y : y + 1, :] * row - beside
        for copy in stores(z, slot):
            copy.start()
        return 0

    lax.fori_loop(0, depth - 2, lambda z, _: write(z, True), 0)
    fill(depth + 1, z_high, edges[1])
    lax.fori_loop(depth - 2, depth, lambda z, _: write(z, False), 0)
    for z in range(depth - SLOTS, depth):
        for copy in stores(z, z % SLOTS):
            copy.wait()


def device_sum(value):
    def exchanged(axis, size, distance):
        return lax.ppermute(value, axis, [(i, i ^ distance) for i in range(size)])

    value = value + exchanged("slab", 32, 1)
    for axis, size, stride in (("slab", 32, 8), ("slab", 32, 2), ("pencil", 4, 1)):
        near, opposite, far = [exchanged(axis, size, d * stride) for d in (1, 2, 3)]
        value = (value + opposite) + (near + far)
    return value


def whole(memory=pltpu.VMEM):
    return pl.BlockSpec(memory_space=memory)


def local(basis, image, material, picked):
    columns, depth, height, width = basis.shape
    count = picked.shape[0]
    slabs, pencils = lax.axis_size("slab"), lax.axis_size("pencil")

    def neighbours(low_face, high_face, axis, size):
        up = [(i, (i + 1) % size) for i in range(size)]
        down = [(j, i) for i, j in up]
        return lax.ppermute(high_face, axis, up), lax.ppermute(low_face, axis, down)

    face = jax.ShapeDtypeStruct((height, columns, width), BF16)
    edge = jax.ShapeDtypeStruct((depth, columns, width), BF16)
    z_first, z_last, y_first, y_last = pl.pallas_call(
        face_kernel,
        in_specs=[whole(pltpu.HBM)],
        out_specs=[whole()] * 4,
        out_shape=[face, face, edge, edge],
        scratch_shapes=[
            pltpu.VMEM((depth, columns, height, width), BF16),
            pltpu.SemaphoreType.DMA((depth,)),
        ],
        compiler_params=pltpu.CompilerParams(vmem_limit_bytes=52 * MIB),
        name="faces",
    )(basis)
    z_low, z_high = neighbours(z_first, z_last, "slab", slabs)
    y_low, y_high = neighbours(y_first, y_last, "pencil", pencils)
    sums, turned = pl.pallas_call(
        gram_kernel,
        in_specs=[whole(pltpu.SMEM), whole(pltpu.HBM), whole(pltpu.HBM)],
        out_specs=[whole()] * 2,
        out_shape=[
            jax.ShapeDtypeStruct((columns + count, columns), F32),
            jax.ShapeDtypeStruct((depth, height, columns, width), BF16),
        ],
        scratch_shapes=[
            pltpu.VMEM((4, columns, height, width), BF16),
            pltpu.VMEM((4, columns, height, width), BF16),
            pltpu.VMEM(((columns + count) * PITCH, width), F32),
            pltpu.SemaphoreType.DMA((4,)),
            pltpu.SemaphoreType.DMA((4,)),
        ],
        compiler_params=pltpu.CompilerParams(vmem_limit_bytes=46 * MIB),
        cost_estimate=pl.CostEstimate(flops=2 * 10**9, bytes_accessed=17 * 10**6, transcendentals=0),
        name="gram",
    )(picked, image, basis)
    faces = (z_low, z_high, y_low, y_high)
    slab, pencil = lax.axis_index("slab"), lax.axis_index("pencil")
    inner = (slab > 0, slab < slabs - 1, pencil > 0, pencil < pencils - 1)
    edges = jnp.stack(inner).astype(jnp.int32)
    grams = jax.ShapeDtypeStruct((columns, columns), F32)
    part = pl.pallas_call(
        inner_kernel,
        in_specs=[whole(pltpu.SMEM)] + [whole()] * 4,
        out_specs=whole(),
        out_shape=grams,
        compiler_params=pltpu.CompilerParams(vmem_limit_bytes=16 * MIB),
        cost_estimate=pl.CostEstimate(flops=10**10, bytes_accessed=10**7, transcendentals=0),
        name="inner",
    )(edges, turned, material, y_low, y_high)
    packed = pl.pallas_call(
        outer_kernel,
        in_specs=[whole(pltpu.SMEM)] + [whole()] * 8,
        out_specs=whole(),
        out_shape=jax.ShapeDtypeStruct((columns, 128), F32),
        scratch_shapes=[pltpu.VMEM(grams.shape, F32)],
        compiler_params=pltpu.CompilerParams(vmem_limit_bytes=16 * MIB),
        name="outer",
    )(edges, sums, part, turned, material, *faces)
    packed = device_sum(packed)
    grid_shape = (count, depth, height, width)
    return pl.pallas_call(
        update_kernel,
        in_specs=[whole(pltpu.SMEM)] + [whole()] * 7,
        out_specs=[whole(pltpu.HBM), whole(pltpu.HBM)],
        out_shape=[jax.ShapeDtypeStruct(grid_shape, F32)] * 2,
        scratch_shapes=[
            pltpu.VMEM((depth + 2, height + 2, count, width), F32),
            pltpu.VMEM((SLOTS, count, STEP, width), F32),
            pltpu.VMEM((SLOTS, count, STEP, width), F32),
            pltpu.SemaphoreType.DMA((SLOTS, 2)),
        ],
        compiler_params=pltpu.CompilerParams(vmem_limit_bytes=20 * MIB),
        name="update",
    )(edges, packed, turned, material, *faces)


def solution(mesh):
    field = P(None, "slab", "pencil", None)
    return jax.shard_map(
        local,
        mesh=mesh,
        in_specs=(field, field, P("slab", "pencil", None), P()),
        out_specs=(field, field),
        check_vma=False,
    )
```
